128 devices in a mesh: dp: 4 (over z_hi, core), blk: 8 (over z_lo, y), ulysses: 4 (over x).
Axes of the slice: x: 4, y: 4, z: 4 (z_hi: 2, z_lo: 2; z = z_hi * 2 + z_lo), core: 2. Of those that a mesh axis runs over, the one named last changes fastest.
Arguments:
- queries: bfloat16 [4, 4096, 2048], P('dp', ('blk', 'ulysses')), may hold values from -8 to 8
- key_vectors: bfloat16 [4, 4096, 512], P('dp', ('blk', 'ulysses')), may hold values from -6 to 6
- value_vectors: bfloat16 [4, 4096, 512], P('dp', ('blk', 'ulysses')), may hold values from -6 to 6
- positions: int32 [4, 4096], P('dp'), may hold values from 0 to 4095, as said below
- out_weight: bfloat16 [2048, 4096], P(('dp', 'blk'), 'ulysses'), may hold values from -0.125 to 0.125
- out_grad: bfloat16 [4, 4096, 4096], P('dp', 'blk', 'ulysses'), may hold values from -6 to 6
Outputs:
- layer_output: bfloat16 [4, 4096, 4096], P('dp', 'blk', 'ulysses')
- query_grad: bfloat16 [4, 4096, 2048], P('dp', ('blk', 'ulysses'))
- key_grad: bfloat16 [4, 4096, 512], P('dp', ('blk', 'ulysses'))
- value_grad: bfloat16 [4, 4096, 512], P('dp', ('blk', 'ulysses'))
- weight_grad: float32 [2048, 4096], P(('dp', 'blk'), 'ulysses')
The draws below stay inside these ranges and needn't reach their ends.
Inputs may be any that keep to these rules, and one draw needn't show every extreme that they name: Every position of a sequence appears once. Tokens come in runs of 256 that hold consecutive positions, each run starting at a multiple of 256; the tokens of one index of blk are two such runs.
All inputs are finite; a program needn't handle non-finite values.
Results may differ from the reference program's by a relative error of at most 0.035.
Values may be sent and summed in bfloat16 or wider, within the bound.
No kernel may reach another device: no remote copies, remote signals or barrier semaphores. Data moves between devices by JAX's collectives and lax.ppermute only.
A program may use at most 192 MiB of HBM per device.

```python
import jax
import jax.numpy as jnp
from jax import lax

D = 4096
HQ = 16
KVH = 4
HD = 128
SEQS = 4
SEQLEN = 4096
SEG = 256


def draw_queries(key, part):
    key = jax.random.fold_in(key, 13)
    group_size = HQ // KVH
    drawn = jnp.clip(jax.random.normal(key, (SEQS, SEQLEN, KVH, group_size, HD)), -6.0, 6.0)
    return drawn.reshape(SEQS, SEQLEN, HQ * HD).astype(jnp.bfloat16)


def draw_key_vectors(key, part):
    key = jax.random.fold_in(key, 11)
    drawn = jnp.clip(jax.random.normal(key, (SEQS, SEQLEN, KVH, HD)), -6.0, 6.0)
    return drawn.reshape(SEQS, SEQLEN, KVH * HD).astype(jnp.bfloat16)


def draw_positions(key, part):
    key = jax.random.fold_in(key, 5)
    run_count = SEQLEN // SEG
    orders = jax.vmap(lambda sub_key: jax.random.permutation(sub_key, run_count))(jax.random.split(key, SEQS))
    token_index = jnp.arange(SEQLEN)
    within = token_index % SEG
    run_slot = token_index // SEG
    return (orders[:, run_slot] * SEG + within[None, :]).astype(jnp.int32)


def shard_levels(key, extent, cuts, least, high):
    level = 1.0
    for dim, shards_of in cuts:
        draws = jax.random.uniform(jax.random.fold_in(jax.random.fold_in(key, 6), dim), (shards_of,), jnp.float32, least / len(cuts), high / len(cuts))
        level = level * jnp.repeat(jnp.exp(draws), extent[dim] // shards_of).reshape((-1,) + (1,) * (len(extent) - 1 - dim))
    return level


def noise(rng, extent, scale, reach, pieces=(), kind=jnp.bfloat16):
    entries = scale * jax.random.normal(rng, extent, jnp.float32)
    if pieces:
        entries = entries * shard_levels(rng, extent, pieces, -0.22, 0.18)
    return jnp.clip(entries, -reach, reach).astype(kind)


def setup_inputs(seed: int = 0) -> dict:
    key_of = jax.random.split(jax.random.key(seed), 7)
    queries = draw_queries(jax.random.fold_in(key_of[6], 71), 0)
    key_vectors = draw_key_vectors(jax.random.fold_in(key_of[6], 71), 0)
    value_vectors = noise(key_of[2], (SEQS, SEQLEN, KVH * HD), 1.0, 6.0, ((0, 4), (1, 32)))
    positions = draw_positions(jax.random.fold_in(key_of[6], 71), 0)
    out_weight = noise(key_of[4], (HQ * HD, D), (HQ * HD) ** -0.5, 0.125, ((0, 32), (1, 4)))
    out_grad = noise(key_of[5], (SEQS, SEQLEN, D), 1.0, 6.0, ((0, 4), (1, 8), (2, 4)))
    return {"queries": queries, "key_vectors": key_vectors, "value_vectors": value_vectors, "positions": positions, "out_weight": out_weight, "out_grad": out_grad}


def attend_pair(pair_items):
    query_block, key_block, value_block, place, grad_block = pair_items
    softmax_scale = HD ** -0.5
    query_wide = query_block.astype(jnp.float32)
    key_wide = key_block.astype(jnp.float32)
    value_wide = value_block.astype(jnp.float32)
    grad_wide = grad_block.astype(jnp.float32)
    scores = jnp.einsum("qgd,kd->gqk", query_wide, key_wide) * softmax_scale
    visible = place[None, :] <= place[:, None]
    scores = jnp.where(visible[None], scores, -jnp.inf)
    row_max = jnp.max(scores, axis=2, keepdims=True)
    exps = jnp.exp(scores - row_max)
    row_total = jnp.sum(exps, axis=2, keepdims=True)
    weights = lax.optimization_barrier(exps.astype(jnp.bfloat16)).astype(jnp.float32)
    summed = jnp.einsum("gqk,kd->qgd", weights, value_wide)
    attended = (summed / jnp.transpose(row_total, (1, 0, 2))).astype(jnp.bfloat16)
    log_total = row_max + jnp.log(row_total)
    probs = jnp.exp(scores - log_total)
    dot_term = jnp.einsum("qgd,qgd->gq", grad_wide, attended.astype(jnp.float32))
    prob_grad = jnp.einsum("qgd,kd->gqk", grad_wide, value_wide)
    score_grad = (probs * (prob_grad - dot_term[..., None]) * softmax_scale).astype(jnp.bfloat16)
    score_grad = lax.optimization_barrier(score_grad).astype(jnp.float32)
    probs_low = lax.optimization_barrier(probs.astype(jnp.bfloat16)).astype(jnp.float32)
    query_part = jnp.einsum("gqk,kd->qgd", score_grad, key_wide).astype(jnp.bfloat16)
    key_part = jnp.einsum("gqk,qgd->kd", score_grad, query_wide).astype(jnp.bfloat16)
    value_part = jnp.einsum("gqk,qgd->kd", probs_low, grad_wide).astype(jnp.bfloat16)
    return attended, query_part, key_part, value_part


def reference(queries, key_vectors, value_vectors, positions, out_weight, out_grad):
    group_size = HQ // KVH
    width = HQ * HD
    grad_flat = out_grad.reshape(SEQS * SEQLEN, D)
    attention_grad = jnp.dot(grad_flat, out_weight.T, preferred_element_type=jnp.float32).astype(jnp.bfloat16)
    attention_grad = attention_grad.reshape(SEQS, SEQLEN, KVH, group_size, HD).transpose(0, 2, 1, 3, 4)
    attention_grad = attention_grad.reshape(SEQS * KVH, SEQLEN, group_size, HD)
    query_pairs = queries.reshape(SEQS, SEQLEN, KVH, group_size, HD).transpose(0, 2, 1, 3, 4)
    query_pairs = query_pairs.reshape(SEQS * KVH, SEQLEN, group_size, HD)
    key_pairs = key_vectors.reshape(SEQS, SEQLEN, KVH, HD).transpose(0, 2, 1, 3).reshape(SEQS * KVH, SEQLEN, HD)
    value_pairs = value_vectors.reshape(SEQS, SEQLEN, KVH, HD).transpose(0, 2, 1, 3).reshape(SEQS * KVH, SEQLEN, HD)
    place_pairs = jnp.repeat(positions, KVH, axis=0)
    attended, query_part, key_part, value_part = lax.map(
        attend_pair, (query_pairs, key_pairs, value_pairs, place_pairs, attention_grad))
    attention = attended.reshape(SEQS, KVH, SEQLEN, group_size, HD).transpose(0, 2, 1, 3, 4)
    attention = attention.reshape(SEQS * SEQLEN, width)
    layer_output = jnp.dot(attention, out_weight, preferred_element_type=jnp.float32).astype(jnp.bfloat16)
    layer_output = layer_output.reshape(SEQS, SEQLEN, D)
    weight_grad = jnp.dot(attention.T, grad_flat, preferred_element_type=jnp.float32)
    query_grad = query_part.reshape(SEQS, KVH, SEQLEN, group_size, HD).transpose(0, 2, 1, 3, 4)
    query_grad = query_grad.reshape(SEQS, SEQLEN, width)
    key_grad = key_part.reshape(SEQS, KVH, SEQLEN, HD).transpose(0, 2, 1, 3).reshape(SEQS, SEQLEN, KVH * HD)
    value_grad = value_part.reshape(SEQS, KVH, SEQLEN, HD).transpose(0, 2, 1, 3).reshape(SEQS, SEQLEN, KVH * HD)
    return layer_output, query_grad, key_grad, value_grad, weight_grad
```

```python
import functools
import math

import jax
import jax.numpy as jnp
from jax import lax
from jax.experimental import pallas as pl
from jax.experimental.pallas import tpu as pltpu
from jax.sharding import Mesh
from jax.sharding import PartitionSpec as P

HD = 128
GROUP = 4
SEG = 256
SCALE = HD ** (-0.5)
LOG2_SCALE = SCALE * math.log2(math.e)
MASKED = -1e30
BF16 = jnp.bfloat16
F32 = jnp.float32
VMEM_LIMIT = 48 * 1024 * 1024
PLANE = ("zhi", "zlo", "y")
BLOCK = ("zlo", "y")


def dot(a, b):
    return jnp.dot(a, b, preferred_element_type=F32)


def dot_nt(a, b):
    return lax.dot_general(a, b, (((1,), (1,)), ((), ())), preferred_element_type=F32)


def diagonal_mask():
    key_index = lax.broadcasted_iota(jnp.int32, (SEG, SEG), 0)
    query_index = lax.broadcasted_iota(jnp.int32, (SEG, SEG), 1)
    return key_index <= query_index


def forward_kernel(
    order_ref, rank_ref, q_ref, kv_ref, att_ref, att_t_ref, lse_ref, q_t, v_t, acc, peak, total
):
    runs = q_ref.shape[0] // SEG
    heads = q_ref.shape[1] // HD
    key_runs = kv_ref.shape[0] // SEG

    q_t[...] = q_ref[...].T

    @pl.loop(0, key_runs)
    def _(j):
        rows = pl.ds(pl.multiple_of(j * SEG, SEG), SEG)
        v_t[j] = kv_ref[rows, HD:].T

    for run in range(runs):
        cols = pl.ds(run * SEG, SEG)
        rank = rank_ref[run]

        def tiles(indexes, first):
            keys = [kv_ref[pl.ds(pl.multiple_of(j * SEG, SEG), SEG), :HD] for j in indexes]
            values = [v_t[j] for j in indexes]
            for h in range(heads):
                queries = q_t[pl.ds(h * HD, HD), cols]
                scores = [dot(k, queries) for k in keys]
                if first:
                    mask = diagonal_mask()
                    scores = [jnp.where(mask, s, MASKED) for s in scores]
                top = functools.reduce(
                    jnp.maximum, [jnp.max(s, axis=0, keepdims=True) for s in scores]
                )
                if not first:
                    old = peak[pl.ds(h, 1), :]
                    top = jnp.maximum(top, old)
                shift = top * LOG2_SCALE
                weights = [jnp.exp2(s * LOG2_SCALE - shift) for s in scores]
                summed = functools.reduce(
                    jnp.add, [jnp.sum(w, axis=0, keepdims=True) for w in weights]
                )
                mixed = functools.reduce(
                    jnp.add, [dot(v, w.astype(BF16)) for v, w in zip(values, weights)]
                )
                if first:
                    total[pl.ds(h, 1), :] = summed
                    acc[pl.ds(h * HD, HD), :] = mixed
                else:
                    factor = jnp.exp2(old * LOG2_SCALE - shift)
                    total[pl.ds(h, 1), :] = total[pl.ds(h, 1), :] * factor + summed
                    acc[pl.ds(h * HD, HD), :] = acc[pl.ds(h * HD, HD), :] * factor + mixed
                peak[pl.ds(h, 1), :] = top

        tiles([order_ref[rank]], True)

        @pl.loop(0, rank // 2)
        def _(pair):
            tiles([order_ref[2 * pair], order_ref[2 * pair + 1]], False)

        @pl.when(rank % 2 == 1)
        def _():
            tiles([order_ref[rank - 1]], False)

        for h in range(heads):
            row_total = total[pl.ds(h, 1), :]
            lse_ref[pl.ds(h, 1), cols] = peak[pl.ds(h, 1), :] * LOG2_SCALE + jnp.log2(row_total)
            out = (acc[pl.ds(h * HD, HD), :] / row_total).astype(BF16)
            att_t_ref[pl.ds(h * HD, HD), cols] = out
            att_ref[cols, pl.ds(h * HD, HD)] = out.T


def attend(order, rank, q, kv):
    rows, width = q.shape
    heads = width // HD
    length = kv.shape[0]
    smem = pl.BlockSpec(memory_space=pltpu.SMEM)
    vmem = pl.BlockSpec(memory_space=pltpu.VMEM)
    return pl.pallas_call(
        forward_kernel,
        name="attention_forward",
        out_shape=(
            jax.ShapeDtypeStruct((rows, width), BF16),
            jax.ShapeDtypeStruct((width, rows), BF16),
            jax.ShapeDtypeStruct((heads, rows), F32),
        ),
        in_specs=[smem, smem, vmem, vmem],
        out_specs=(vmem, vmem, vmem),
        scratch_shapes=[
            pltpu.VMEM((width, rows), BF16),
            pltpu.VMEM((length // SEG, HD, SEG), BF16),
            pltpu.VMEM((width, SEG), F32),
            pltpu.VMEM((8, SEG), F32),
            pltpu.VMEM((8, SEG), F32),
        ],
        compiler_params=pltpu.CompilerParams(vmem_limit_bytes=VMEM_LIMIT),
        cost_estimate=pl.CostEstimate(
            flops=4 * rows * length * width,
            bytes_accessed=2 * (3 * rows * width + length * 2 * HD),
            transcendentals=rows * length * heads,
        ),
    )(order, rank, q, kv)


def backward_kernel(
    rank_ref,
    key_rank_ref,
    q_ref,
    kv_ref,
    grad_t_ref,
    att_t_ref,
    lse_ref,
    dq_ref,
    dkv_ref,
    q_t,
    grad,
    delta,
    dq_t,
    dk,
    dv,
):
    runs = q_ref.shape[0] // SEG
    heads = q_ref.shape[1] // HD
    key_runs = kv_ref.shape[0] // SEG

    q_t[...] = q_ref[...].T
    grad[...] = grad_t_ref[...].T
    dq_t[...] = jnp.zeros_like(dq_t)
    for h in range(heads):
        part = pl.ds(h * HD, HD)
        delta[pl.ds(h, 1), :] = jnp.sum(
            grad_t_ref[part, :].astype(F32) * att_t_ref[part, :].astype(F32),
            axis=0,
            keepdims=True,
        )

    @pl.loop(0, key_runs)
    def _(j):
        rows = pl.ds(pl.multiple_of(j * SEG, SEG), SEG)
        key_rank = key_rank_ref[j]
        dk[...] = jnp.zeros_like(dk)
        dv[...] = jnp.zeros_like(dv)

        def tile(run, masked):
            cols = pl.ds(run * SEG, SEG)
            keys = kv_ref[rows, :HD]
            values = kv_ref[rows, HD:]
            keys_t = keys.T
            dk_now = dk[...]
            dv_now = dv[...]
            for h in range(heads):
                part = pl.ds(h * HD, HD)
                scores = dot(keys, q_t[part, cols])
                probs = jnp.exp2(scores * LOG2_SCALE - lse_ref[pl.ds(h, 1), cols])
                if masked:
                    probs = jnp.where(diagonal_mask(), probs, 0.0)
                prob_grad = dot(values, grad_t_ref[part, cols])
                score_grad = (probs * (prob_grad - delta[pl.ds(h, 1), cols])).astype(BF16)
                dv_now = dv_now + dot(probs.astype(BF16), grad[cols, part])
                dk_now = dk_now + dot(score_grad, q_ref[cols, part])
                dq_t[part, cols] += dot(keys_t, score_grad)
            dk[...] = dk_now
            dv[...] = dv_now

        for run in range(runs):
            pl.when(key_rank < rank_ref[run])(functools.partial(tile, run, False))
            pl.when(key_rank == rank_ref[run])(functools.partial(tile, run, True))
        dkv_ref[rows, :HD] = (dk[...] * SCALE).astype(BF16)
        dkv_ref[rows, HD:] = dv[...].astype(BF16)

    for run in range(runs):
        cols = pl.ds(run * SEG, SEG)
        for h in range(heads):
            part = pl.ds(h * HD, HD)
            dq_ref[cols, part] = (dq_t[part, cols] * SCALE).astype(BF16).T


def attend_back(rank, key_rank, q, kv, grad_t, att_t, lse):
    rows, width = q.shape
    heads = width // HD
    length = kv.shape[0]
    smem = pl.BlockSpec(memory_space=pltpu.SMEM)
    vmem = pl.BlockSpec(memory_space=pltpu.VMEM)
    return pl.pallas_call(
        backward_kernel,
        name="attention_backward",
        out_shape=(
            jax.ShapeDtypeStruct((rows, width), BF16),
            jax.ShapeDtypeStruct((length, 2 * HD), BF16),
        ),
        in_specs=[smem, smem] + [vmem] * 5,
        out_specs=(vmem, vmem),
        scratch_shapes=[
            pltpu.VMEM((width, rows), BF16),
            pltpu.VMEM((rows, width), BF16),
            pltpu.VMEM((8, rows), F32),
            pltpu.VMEM((width, rows), F32),
            pltpu.VMEM((SEG, HD), F32),
            pltpu.VMEM((SEG, HD), F32),
        ],
        compiler_params=pltpu.CompilerParams(vmem_limit_bytes=VMEM_LIMIT),
        cost_estimate=pl.CostEstimate(
            flops=10 * rows * length * width,
            bytes_accessed=2 * (4 * rows * width + 2 * length * 2 * HD),
            transcendentals=rows * length * heads,
        ),
    )(rank, key_rank, q, kv, grad_t, att_t, lse)


def pack_kernel(q_ref, k_ref, v_ref, out_ref):
    parts, _, total = out_ref.shape
    width = total - 2 * HD
    for i in range(parts):
        out_ref[i, :, :width] = q_ref[0, :, pl.ds(i * width, width)]
        out_ref[i, :, width : width + HD] = k_ref[0, :, pl.ds(i * HD, HD)]
        out_ref[i, :, width + HD :] = v_ref[0, :, pl.ds(i * HD, HD)]


def pack(queries, key_vectors, value_vectors):
    own = queries.shape[1]
    parts = key_vectors.shape[2] // HD
    width = queries.shape[2] // parts
    return pl.pallas_call(
        pack_kernel,
        name="pack_heads",
        out_shape=jax.ShapeDtypeStruct((parts, own, width + 2 * HD), BF16),
    )(queries, key_vectors, value_vectors)


def finish_kernel(source_ref, *refs):
    pieces, dkv_ref, (dq_ref, dk_ref, dv_ref) = refs[:-4], refs[-4], refs[-3:]
    width = pieces[0].shape[1]
    for i, piece in enumerate(pieces):
        columns = pl.ds(pl.multiple_of(source_ref[i] * width, width), width)
        dq_ref[0, :, columns] = piece[...]
    blocks, parts = dkv_ref.shape[:2]
    for u in range(parts):
        total = dkv_ref[0, u].astype(F32)
        for b in range(1, blocks):
            total = total + dkv_ref[b, u].astype(F32)
        total = total.astype(BF16)
        dk_ref[0, :, pl.ds(u * HD, HD)] = total[:, :HD]
        dv_ref[0, :, pl.ds(u * HD, HD)] = total[:, HD:]


def finish(source, pieces, dkv):
    own, width = pieces[0].shape
    parts = len(pieces)
    smem = pl.BlockSpec(memory_space=pltpu.SMEM)
    vmem = pl.BlockSpec(memory_space=pltpu.VMEM)
    return pl.pallas_call(
        finish_kernel,
        name="gather_gradients",
        in_specs=[smem] + [vmem] * (parts + 1),
        out_specs=(vmem, vmem, vmem),
        out_shape=(
            jax.ShapeDtypeStruct((1, own, parts * width), BF16),
            jax.ShapeDtypeStruct((1, own, parts * HD), BF16),
            jax.ShapeDtypeStruct((1, own, parts * HD), BF16),
        ),
        compiler_params=pltpu.CompilerParams(vmem_limit_bytes=VMEM_LIMIT),
    )(source, *pieces, dkv)


def exchange(array, axes):
    return lax.all_to_all(array, axes, split_axis=0, concat_axis=0, tiled=True)


def shift(array, axis, by):
    length = lax.axis_size(axis)
    return lax.ppermute(array, axis, [(i, (i + by) % length) for i in range(length)])


def pick(array, index):
    return lax.dynamic_index_in_dim(array, index, 0, keepdims=False)


def put(array, piece, index):
    return lax.dynamic_update_index_in_dim(array, piece, index, 0)


def swap_pairs(by):
    pairs = []
    for zhi in range(2):
        for core in range(2):
            for y in range(4):
                for x in range(4):
                    source = ((zhi * 2 + core) * 4 + y) * 4 + x
                    target = (((x % 2) * 2 + x // 2) * 4 + (y + by) % 4) * 4 + zhi * 2 + core
                    pairs.append((source, target))
    return pairs


def swap(array, by):
    return lax.ppermute(array, ("zhi", "core", "y", "x"), swap_pairs(by))


def swap_back(array):
    return lax.ppermute(array, ("zhi", "core", "y", "x"), [(b, a) for a, b in swap_pairs(0)])


def after(array, *others):
    return lax.optimization_barrier((array,) + others)[0]


def shards(queries, key_vectors, value_vectors, positions, out_weight, out_grad):
    x = lax.axis_index("x")
    y = lax.axis_index("y")
    z = lax.axis_index(("zhi", "zlo"))
    core = lax.axis_index("core")
    blk = lax.axis_index(BLOCK)
    xs = lax.axis_size("x")
    own = queries.shape[1]
    width = queries.shape[2] // xs
    blocks = lax.axis_size(BLOCK)
    rows = own * xs
    columns = out_grad.shape[2]

    key_rank = positions[0, ::SEG] // SEG
    count = key_rank.shape[0]
    index = jnp.arange(count, dtype=jnp.int32)
    order = jnp.sum(
        jnp.where(key_rank[None, :] == index[:, None], index[None, :], 0), axis=1
    ).astype(jnp.int32)
    rank = lax.dynamic_slice_in_dim(key_rank, blk * (rows // SEG), rows // SEG)

    og = lax.all_gather(out_grad[0], "x", axis=0)

    along_y = jnp.zeros((4,) + out_weight.shape, BF16)
    for d in range(4):
        along_y = put(along_y, swap(out_weight, d), (y - d) % 4)
    along_z = put(jnp.zeros((4,) + along_y.shape, BF16), along_y, z)
    for d in range(1, 4):
        along_z = put(along_z, shift(along_y, ("zhi", "zlo"), d), (z - d) % 4)
    weight = put(jnp.zeros((2,) + along_z.shape, BF16), along_z, core)
    weight = put(weight, shift(along_z, "core", 1), 1 - core)
    weight = weight.reshape(xs, width, columns)

    qkv = exchange(pack(queries, key_vectors, value_vectors), "x").reshape(rows, width + 2 * HD)
    q, kv_block = qkv[:, :width], qkv[:, width:]

    kv = exchange(jnp.broadcast_to(kv_block[None], (blocks,) + kv_block.shape), BLOCK)
    kv = kv.reshape(blocks * rows, 2 * HD)

    att, att_t, lse = attend(order, rank, q, kv)

    og_half = og.reshape(2, 2, rows, columns)

    def weight_part(half):
        return jnp.einsum("ft,ztc->zfc", att_t, pick(og_half, half), preferred_element_type=F32)

    wg_got = shift(weight_part(1 - core).astype(BF16), "core", 1)
    wg_half = (weight_part(core) + wg_got.astype(F32)).astype(BF16)
    wg_half = wg_half.reshape(2 * blocks, width // blocks, columns)
    wg_parts = exchange(wg_half, PLANE)
    weight_grad = swap_back(jnp.sum(wg_parts.astype(F32), axis=0))

    grad_t = jnp.einsum("gfc,gtc->ft", weight, og, preferred_element_type=F32).astype(BF16)

    lo = jnp.einsum("tf,gfc->gtc", att, weight, preferred_element_type=F32).astype(BF16)
    layer_output = lax.psum_scatter(lo, "x", scatter_dimension=0, tiled=True)

    grad_t = after(grad_t, wg_half, lo)
    dq, dkv = attend_back(rank, key_rank, q, kv, grad_t, att_t, lse)

    dq_parts = dq.reshape(xs, own, width)
    pieces = [pick(dq_parts, x)]
    for d in range(1, xs):
        pieces.append(shift(pick(dq_parts, (x + d) % xs), "x", d))
    source = jnp.stack([(x - d) % xs for d in range(xs)]).astype(jnp.int32)
    dkv_got = exchange(dkv.reshape(blocks * xs, own, 2 * HD), BLOCK + ("x",))
    dkv_got = dkv_got.reshape(blocks, xs, own, 2 * HD)
    query_grad, key_grad, value_grad = finish(source, pieces, dkv_got)
    return (layer_output, query_grad, key_grad, value_grad, weight_grad)


def solution(mesh):
    split = Mesh(mesh.devices.reshape(2, 2, 2, 4, 4), ("zhi", "core", "zlo", "y", "x"))
    dp = ("zhi", "core")
    tokens = P(dp, ("zlo", "y", "x"), None)
    weight = P(("zhi", "core", "zlo", "y"), "x")
    columns = P(dp, BLOCK, "x")
    return jax.shard_map(
        shards,
        mesh=split,
        in_specs=(tokens, tokens, tokens, P(dp, None), weight, columns),
        out_specs=(columns, tokens, tokens, tokens, weight),
        check_vma=False,
    )
```

```python
import functools
import math

import jax
import jax.numpy as jnp
from jax import lax
from jax.experimental import pallas as pl
from jax.experimental.pallas import tpu as pltpu
from jax.sharding import Mesh
from jax.sharding import PartitionSpec as P

HD = 128
GROUP = 4
SEG = 256
SCALE = HD ** (-0.5)
LOG2_SCALE = SCALE * math.log2(math.e)
MASKED = -1e30
BF16 = jnp.bfloat16
F32 = jnp.float32
VMEM_LIMIT = 48 * 1024 * 1024
SHORT = pl.CostEstimate(flops=1, bytes_accessed=1, transcendentals=0)
PLANE = ("zhi", "zlo", "y")
BLOCK = ("zlo", "y")


def dot(a, b):
    return jnp.dot(a, b, preferred_element_type=F32)


def dot_nt(a, b):
    return lax.dot_general(a, b, (((1,), (1,)), ((), ())), preferred_element_type=F32)


def diagonal_mask():
    key_index = lax.broadcasted_iota(jnp.int32, (SEG, SEG), 0)
    query_index = lax.broadcasted_iota(jnp.int32, (SEG, SEG), 1)
    return key_index <= query_index


def pipeline(units, score, soften, mix):
    now = score(units[0])
    state = None
    for i in range(len(units) + 1):
        following = score(units[i + 1]) if i + 1 < len(units) else None
        if state is not None:
            mix(units[i - 1], state)
        if i < len(units):
            state = soften(units[i], now)
        now = following


def forward_kernel(order_ref, rank_ref, source_ref, *refs):
    pieces, (kv_ref, q_ref, att_t_ref, lse_ref, q_t, v_t, acc, peak, total) = refs[:-9], refs[-9:]
    own = pieces[0].shape[0]
    for i, piece in enumerate(pieces):
        place = pl.multiple_of(source_ref[i] * own, own)
        q_ref[pl.ds(place, own), :] = piece[...]
    runs = q_ref.shape[0] // SEG
    heads = q_ref.shape[1] // HD
    key_runs = kv_ref.shape[0] // SEG

    q_t[...] = q_ref[...].T

    @pl.loop(0, key_runs)
    def _(j):
        rows = pl.ds(pl.multiple_of(j * SEG, SEG), SEG)
        v_t[j] = kv_ref[rows, HD:].T

    for run in range(runs):
        cols = pl.ds(run * SEG, SEG)
        rank = rank_ref[run]

        def tiles(groups, first):
            units = [(g, h) for g in range(len(groups)) for h in range(heads)]
            keys = [
                [kv_ref[pl.ds(pl.multiple_of(j * SEG, SEG), SEG), :HD] for j in group]
                for group in groups
            ]
            values = [[v_t[j] for j in group] for group in groups]

            def score(unit):
                g, h = unit
                queries = q_t[pl.ds(h * HD, HD), cols]
                return [dot(k, queries) for k in keys[g]]

            def soften(unit, scores):
                g, h = unit
                if first and g == 0:
                    mask = diagonal_mask()
                    scores = [jnp.where(mask, s, MASKED) for s in scores]
                top = functools.reduce(
                    jnp.maximum, [jnp.max(s, axis=0, keepdims=True) for s in scores]
                )
                factor = None
                if not (first and g == 0):
                    old = peak[pl.ds(h, 1), :]
                    top = jnp.maximum(top, old)
                    factor = jnp.exp2((old - top) * LOG2_SCALE)
                peak[pl.ds(h, 1), :] = top
                shift = top * LOG2_SCALE
                weights = [jnp.exp2(s * LOG2_SCALE - shift) for s in scores]
                summed = functools.reduce(
                    jnp.add, [jnp.sum(w, axis=0, keepdims=True) for w in weights]
                )
                return factor, summed, [w.astype(BF16) for w in weights]

            def mix(unit, state):
                g, h = unit
                factor, summed, weights = state
                mixed = functools.reduce(
                    jnp.add, [dot(v, w) for v, w in zip(values[g], weights)]
                )
                if factor is None:
                    total[pl.ds(h, 1), :] = summed
                    acc[pl.ds(h * HD, HD), :] = mixed
                else:
                    total[pl.ds(h, 1), :] = total[pl.ds(h, 1), :] * factor + summed
                    acc[pl.ds(h * HD, HD), :] = acc[pl.ds(h * HD, HD), :] * factor + mixed

            pipeline(units, score, soften, mix)

        rest = rank % 4
        for left in range(4):

            @pl.when(rest == left)
            def _():
                groups = [[order_ref[rank]]]
                if left >= 2:
                    groups.append([order_ref[rank - 1], order_ref[rank - 2]])
                if left % 2:
                    groups.append([order_ref[rank - left]])
                tiles(groups, True)

        @pl.loop(0, rank // 4)
        def _(quad):
            start = 4 * quad
            tiles(
                [
                    [order_ref[start], order_ref[start + 1]],
                    [order_ref[start + 2], order_ref[start + 3]],
                ],
                False,
            )

        for h in range(heads):
            row_total = total[pl.ds(h, 1), :]
            lse_ref[pl.ds(h, 1), cols] = peak[pl.ds(h, 1), :] * LOG2_SCALE + jnp.log2(row_total)
            out = (acc[pl.ds(h * HD, HD), :] / row_total).astype(BF16)
            att_t_ref[pl.ds(h * HD, HD), cols] = out


def attend(order, rank, source, pieces, kv):
    own, width = pieces[0].shape
    rows = own * len(pieces)
    heads = width // HD
    length = kv.shape[0]
    smem = pl.BlockSpec(memory_space=pltpu.SMEM)
    vmem = pl.BlockSpec(memory_space=pltpu.VMEM)
    return pl.pallas_call(
        forward_kernel,
        name="attention_forward",
        out_shape=(
            jax.ShapeDtypeStruct((rows, width), BF16),
            jax.ShapeDtypeStruct((width, rows), BF16),
            jax.ShapeDtypeStruct((heads, rows), F32),
        ),
        in_specs=[smem, smem, smem] + [vmem] * (len(pieces) + 1),
        out_specs=(vmem, vmem, vmem),
        scratch_shapes=[
            pltpu.VMEM((width, rows), BF16),
            pltpu.VMEM((length // SEG, HD, SEG), BF16),
            pltpu.VMEM((width, SEG), F32),
            pltpu.VMEM((8, SEG), F32),
            pltpu.VMEM((8, SEG), F32),
        ],
        compiler_params=pltpu.CompilerParams(vmem_limit_bytes=VMEM_LIMIT),
        cost_estimate=pl.CostEstimate(
            flops=4 * rows * length * width,
            bytes_accessed=2 * (3 * rows * width + length * 2 * HD),
            transcendentals=rows * length * heads,
        ),
    )(order, rank, source, *pieces, kv)


def backward_kernel(
    rank_ref,
    key_rank_ref,
    q_ref,
    kv_ref,
    grad_t_ref,
    att_t_ref,
    lse_ref,
    dq_ref,
    dkv_ref,
    q_t,
    grad,
    delta,
    dq_t,
    dk,
    dv,
):
    runs = q_ref.shape[0] // SEG
    heads = q_ref.shape[1] // HD
    key_runs = kv_ref.shape[0] // SEG

    q_t[...] = q_ref[...].T
    grad[...] = grad_t_ref[...].T
    dq_t[...] = jnp.zeros_like(dq_t)
    for h in range(heads):
        part = pl.ds(h * HD, HD)
        delta[pl.ds(h, 1), :] = jnp.sum(
            grad_t_ref[part, :].astype(F32) * att_t_ref[part, :].astype(F32),
            axis=0,
            keepdims=True,
        )

    @pl.loop(0, key_runs)
    def _(j):
        rows = pl.ds(pl.multiple_of(j * SEG, SEG), SEG)
        key_rank = key_rank_ref[j]
        dk[...] = jnp.zeros_like(dk)
        dv[...] = jnp.zeros_like(dv)

        def tile(chosen, masked):
            keys = kv_ref[rows, :HD]
            values = kv_ref[rows, HD:]
            keys_t = keys.T
            sums = [dk[...], dv[...]]
            units = [(run, h) for run in chosen for h in range(heads)]

            def place(unit):
                return pl.ds(unit[1] * HD, HD), pl.ds(unit[0] * SEG, SEG)

            def score(unit):
                part, cols = place(unit)
                return dot(keys, q_t[part, cols]), dot(values, grad_t_ref[part, cols])

            def soften(unit, state):
                scores, prob_grad = state
                _, cols = place(unit)
                row = pl.ds(unit[1], 1)
                probs = jnp.exp2(scores * LOG2_SCALE - lse_ref[row, cols])
                if masked:
                    probs = jnp.where(diagonal_mask(), probs, 0.0)
                score_grad = (probs * (prob_grad - delta[row, cols])).astype(BF16)
                return probs.astype(BF16), score_grad

            def mix(unit, state):
                probs, score_grad = state
                part, cols = place(unit)
                dq_t[part, cols] += dot(keys_t, score_grad)
                sums[0] = sums[0] + dot(score_grad, q_ref[cols, part])
                sums[1] = sums[1] + dot(probs, grad[cols, part])

            pipeline(units, score, soften, mix)
            dk[...] = sums[0]
            dv[...] = sums[1]

        whole = [key_rank < rank_ref[run] for run in range(runs)]
        every = functools.reduce(jnp.logical_and, whole)
        pl.when(every)(functools.partial(tile, range(runs), False))
        for run in range(runs):
            alone = jnp.logical_and(whole[run], jnp.logical_not(every))
            pl.when(alone)(functools.partial(tile, [run], False))
            pl.when(key_rank == rank_ref[run])(functools.partial(tile, [run], True))
        dkv_ref[rows, :HD] = (dk[...] * SCALE).astype(BF16)
        dkv_ref[rows, HD:] = dv[...].astype(BF16)

    for run in range(runs):
        cols = pl.ds(run * SEG, SEG)
        for h in range(heads):
            part = pl.ds(h * HD, HD)
            dq_ref[cols, part] = (dq_t[part, cols] * SCALE).astype(BF16).T


def attend_back(rank, key_rank, q, kv, grad_t, att_t, lse):
    rows, width = q.shape
    heads = width // HD
    length = kv.shape[0]
    smem = pl.BlockSpec(memory_space=pltpu.SMEM)
    vmem = pl.BlockSpec(memory_space=pltpu.VMEM)
    return pl.pallas_call(
        backward_kernel,
        name="attention_backward",
        out_shape=(
            jax.ShapeDtypeStruct((rows, width), BF16),
            jax.ShapeDtypeStruct((length, 2 * HD), BF16),
        ),
        in_specs=[smem, smem] + [vmem] * 5,
        out_specs=(vmem, vmem),
        scratch_shapes=[
            pltpu.VMEM((width, rows), BF16),
            pltpu.VMEM((rows, width), BF16),
            pltpu.VMEM((8, rows), F32),
            pltpu.VMEM((width, rows), F32),
            pltpu.VMEM((SEG, HD), F32),
            pltpu.VMEM((SEG, HD), F32),
        ],
        compiler_params=pltpu.CompilerParams(vmem_limit_bytes=VMEM_LIMIT),
        cost_estimate=pl.CostEstimate(
            flops=10 * rows * length * width,
            bytes_accessed=2 * (4 * rows * width + 2 * length * 2 * HD),
            transcendentals=rows * length * heads,
        ),
    )(rank, key_rank, q, kv, grad_t, att_t, lse)


def pack_kernel(target_ref, q_ref, k_ref, v_ref, kv_ref, *pieces):
    width = pieces[0].shape[1]
    for i, piece in enumerate(pieces):
        columns = pl.ds(pl.multiple_of(target_ref[i] * width, width), width)
        piece[...] = q_ref[0, :, columns]
        kv_ref[i, :, :HD] = k_ref[0, :, pl.ds(i * HD, HD)]
        kv_ref[i, :, HD:] = v_ref[0, :, pl.ds(i * HD, HD)]


def pack(target, queries, key_vectors, value_vectors):
    own = queries.shape[1]
    parts = key_vectors.shape[2] // HD
    width = queries.shape[2] // parts
    smem = pl.BlockSpec(memory_space=pltpu.SMEM)
    vmem = pl.BlockSpec(memory_space=pltpu.VMEM)
    return pl.pallas_call(
        pack_kernel,
        name="pack_heads",
        in_specs=[smem, vmem, vmem, vmem],
        out_specs=(vmem,) * (parts + 1),
        out_shape=(jax.ShapeDtypeStruct((parts, own, 2 * HD), BF16),)
        + (jax.ShapeDtypeStruct((own, width), BF16),) * parts,
    )(target, queries, key_vectors, value_vectors)


def choose(mine, first, second, run):
    pl.when(mine)(functools.partial(run, first))
    pl.when(jnp.logical_not(mine))(functools.partial(run, second))


def grad_kernel(group_ref, core_ref, mine_ref, other_ref, *refs):
    *pieces, first, second, out_ref, total = refs
    for i in range(len(pieces) + 1):
        group = group_ref[i]

        def product(weight, i=i, group=group):
            rows = weight[group % 2]
            if i < len(pieces):
                term = dot_nt(rows, pieces[i][0])
            else:
                term = jnp.concatenate([dot_nt(rows, first[...]), dot_nt(rows, second[...])], axis=1)
            total[...] = term if i == 0 else total[...] + term

        choose(group // 2 == core_ref[0], mine_ref, other_ref, product)
    out_ref[...] = total[...].astype(BF16)


def project_back(groups, core, mine, other, pieces):
    width, rows = mine.shape[1], pieces[0].shape[1]
    smem = pl.BlockSpec(memory_space=pltpu.SMEM)
    vmem = pl.BlockSpec(memory_space=pltpu.VMEM)
    return pl.pallas_call(
        grad_kernel,
        name="attention_grad",
        in_specs=[smem, smem] + [vmem] * (2 + len(pieces)),
        out_specs=vmem,
        out_shape=jax.ShapeDtypeStruct((width, rows), BF16),
        scratch_shapes=[pltpu.VMEM((width, rows), F32)],
        compiler_params=pltpu.CompilerParams(vmem_limit_bytes=VMEM_LIMIT),
        cost_estimate=SHORT,
    )(groups, core, mine, other, *pieces)


def weight_grad_kernel(group_ref, core_ref, att_t_ref, *refs):
    *pieces, first, second, mine_ref, other_ref = refs
    half = first.shape[0]
    for i in range(len(pieces) + 1):
        group = group_ref[i]

        def product(out, i=i, group=group):
            if i < len(pieces):
                term = dot(att_t_ref[...], pieces[i][0])
            else:
                term = dot(att_t_ref[:, :half], first[...]) + dot(att_t_ref[:, half:], second[...])
            out[group % 2] = term.astype(BF16)

        choose(group // 2 == core_ref[0], mine_ref, other_ref, product)


def weight_grad_parts(groups, core, att_t, pieces):
    count = groups.shape[0]
    out = jax.ShapeDtypeStruct((count // 2, att_t.shape[0], pieces[0].shape[2]), BF16)
    smem = pl.BlockSpec(memory_space=pltpu.SMEM)
    vmem = pl.BlockSpec(memory_space=pltpu.VMEM)
    return pl.pallas_call(
        weight_grad_kernel,
        name="weight_grad_parts",
        in_specs=[smem, smem] + [vmem] * (1 + len(pieces)),
        out_specs=(vmem, vmem),
        out_shape=(out, out),
        compiler_params=pltpu.CompilerParams(vmem_limit_bytes=VMEM_LIMIT),
        cost_estimate=SHORT,
    )(groups, core, att_t, *pieces)


def output_kernel(group_ref, core_ref, mine_ref, other_ref, att_t_ref, *refs):
    *outs, first, second, att = refs
    half = first.shape[0]
    att[...] = att_t_ref[...].T
    for i in range(len(outs) + 1):
        group = group_ref[i]

        def product(weight, i=i, group=group):
            term = dot(att[...], weight[group % 2])
            if i < len(outs):
                outs[i][...] = term.astype(outs[i].dtype)
            else:
                first[...] = term[:half].astype(BF16)
                second[...] = term[half:].astype(BF16)

        choose(group // 2 == core_ref[0], mine_ref, other_ref, product)


def project(groups, core, mine, other, att_t):
    count = groups.shape[0]
    width, rows = att_t.shape
    columns = mine.shape[2]
    smem = pl.BlockSpec(memory_space=pltpu.SMEM)
    vmem = pl.BlockSpec(memory_space=pltpu.VMEM)
    return pl.pallas_call(
        output_kernel,
        name="layer_output_parts",
        in_specs=[smem, smem] + [vmem] * 3,
        out_specs=(vmem,) * (count + 1),
        out_shape=(
            jax.ShapeDtypeStruct((rows, columns), F32),
            jax.ShapeDtypeStruct((rows, columns), BF16),
            jax.ShapeDtypeStruct((rows, columns), BF16),
            jax.ShapeDtypeStruct((rows // 2, columns), BF16),
            jax.ShapeDtypeStruct((rows // 2, columns), BF16),
        ),
        scratch_shapes=[pltpu.VMEM((rows, width), BF16)],
        compiler_params=pltpu.CompilerParams(vmem_limit_bytes=VMEM_LIMIT),
        cost_estimate=SHORT,
    )(groups, core, mine, other, att_t)


def finish_kernel(source_ref, *refs):
    pieces, dkv_ref, (dq_ref, dk_ref, dv_ref) = refs[:-4], refs[-4], refs[-3:]
    width = pieces[0].shape[1]
    for i, piece in enumerate(pieces):
        columns = pl.ds(pl.multiple_of(source_ref[i] * width, width), width)
        dq_ref[0, :, columns] = piece[...]
    blocks, parts = dkv_ref.shape[:2]
    for u in range(parts):
        total = dkv_ref[0, u].astype(F32)
        for b in range(1, blocks):
            total = total + dkv_ref[b, u].astype(F32)
        total = total.astype(BF16)
        dk_ref[0, :, pl.ds(u * HD, HD)] = total[:, :HD]
        dv_ref[0, :, pl.ds(u * HD, HD)] = total[:, HD:]


def finish(source, pieces, dkv):
    own, width = pieces[0].shape
    parts = len(pieces)
    smem = pl.BlockSpec(memory_space=pltpu.SMEM)
    vmem = pl.BlockSpec(memory_space=pltpu.VMEM)
    return pl.pallas_call(
        finish_kernel,
        name="gather_gradients",
        in_specs=[smem] + [vmem] * (parts + 1),
        out_specs=(vmem, vmem, vmem),
        out_shape=(
            jax.ShapeDtypeStruct((1, own, parts * width), BF16),
            jax.ShapeDtypeStruct((1, own, parts * HD), BF16),
            jax.ShapeDtypeStruct((1, own, parts * HD), BF16),
        ),
        compiler_params=pltpu.CompilerParams(vmem_limit_bytes=VMEM_LIMIT),
    )(source, *pieces, dkv)


def exchange(array, axes):
    return lax.all_to_all(array, axes, split_axis=0, concat_axis=0, tiled=True)


def shift(array, axis, by):
    length = lax.axis_size(axis)
    return lax.ppermute(array, axis, [(i, (i + by) % length) for i in range(length)])


def pick(array, index):
    return lax.dynamic_index_in_dim(array, index, 0, keepdims=False)


def put(array, piece, index):
    return lax.dynamic_update_index_in_dim(array, piece, index, 0)


def spread(array, count):
    return jnp.broadcast_to(array[None], (count,) + array.shape).reshape(
        (count * array.shape[0],) + array.shape[1:]
    )


def swap_pairs():
    pairs = []
    for zhi in range(2):
        for core in range(2):
            for x in range(4):
                source = (zhi * 2 + core) * 4 + x
                target = ((x % 2) * 2 + x // 2) * 4 + zhi * 2 + core
                pairs.append((source, target))
    return pairs


def swap(array):
    return lax.ppermute(array, ("zhi", "core", "x"), swap_pairs())


def swap_back(array):
    return lax.ppermute(array, ("zhi", "core", "x"), [(b, a) for a, b in swap_pairs()])


def flip(array, by):
    return lax.ppermute(array, "x", [(i, i ^ by) for i in range(4)])


def after(array, *others):
    return lax.optimization_barrier((array,) + others)[0]


def shards(queries, key_vectors, value_vectors, positions, out_weight, out_grad):
    x = lax.axis_index("x")
    core = lax.axis_index("core")
    blk = lax.axis_index(BLOCK)
    xs = lax.axis_size("x")
    own = queries.shape[1]
    width = queries.shape[2] // xs
    blocks = lax.axis_size(BLOCK)
    rows = own * xs
    columns = out_grad.shape[2]

    key_rank = positions[0, ::SEG] // SEG
    count = key_rank.shape[0]
    index = jnp.arange(count, dtype=jnp.int32)
    order = jnp.sum(
        jnp.where(key_rank[None, :] == index[:, None], index[None, :], 0), axis=1
    ).astype(jnp.int32)
    rank = lax.dynamic_slice_in_dim(key_rank, blk * (rows // SEG), rows // SEG)

    steps = jnp.arange(xs, dtype=jnp.int32)
    target, source = (x + steps) % xs, (x - steps) % xs

    weight_swapped = swap(out_weight)
    kv_parts, *q_parts = pack(target, queries, key_vectors, value_vectors)
    q_pieces = q_parts[:1] + [shift(q_parts[d], "x", d) for d in range(1, xs)]
    kv = exchange(spread(kv_parts, blocks), BLOCK + ("x",)).reshape(blocks * rows, 2 * HD)

    near = jnp.stack([x, x ^ 1, x ^ 3, x ^ 2]).astype(jnp.int32)
    half = rows // 2
    og_own = after(out_grad, kv, weight_swapped, *q_pieces)
    og_1, og_3 = flip(og_own, 1), flip(og_own, 3)

    weight_swapped = after(weight_swapped, kv, *q_pieces)
    weight_half = exchange(spread(weight_swapped, 2 * blocks), PLANE)

    q, att_t, lse = attend(order, rank, source, q_pieces, kv)

    og_1, og_3, _ = lax.optimization_barrier((og_1, og_3, att_t))
    og = [out_grad, og_1, og_3, flip(og_1[0, :half], 3), flip(og_3[0, half:], 1)]

    weight_mine = after(weight_half, att_t).reshape(2, width, columns)
    weight_other = shift(weight_mine, "core", 1)

    cores = core.astype(jnp.int32).reshape(1)
    wg_mine, wg_sent = weight_grad_parts(near, cores, att_t, og)
    grad_t = project_back(near, cores, weight_mine, weight_other, og)

    wg_got = after(shift(wg_sent, "core", 1), grad_t)
    wg_half = (wg_mine.astype(F32) + wg_got.astype(F32)).astype(BF16)
    wg_half = wg_half.reshape(2 * blocks, width // blocks, columns)
    wg_parts = exchange(wg_half, PLANE)
    weight_grad = swap_back(jnp.sum(wg_parts.astype(F32), axis=0))

    lo, lo_1, lo_3, lo_first, lo_second = project(near, cores, weight_mine, weight_other, att_t)
    lo_3 = lo_3.at[:half].add(flip(lo_first, 1))
    lo_1 = lo_1.at[half:].add(flip(lo_second, 3))
    lo = lo + flip(lo_1, 1).astype(F32) + flip(lo_3, 3).astype(F32)
    layer_output = lo.astype(BF16)[None]

    grad_t = after(grad_t, wg_half, lo_1, lo_3)
    dq, dkv = attend_back(rank, key_rank, q, kv, grad_t, att_t, lse)

    dkv = after(dkv, layer_output)
    dq_parts = dq.reshape(xs, own, width)
    pieces = [pick(dq_parts, x)]
    for d in range(1, xs):
        pieces.append(shift(pick(dq_parts, (x + d) % xs), "x", d))
    dkv_got = exchange(dkv.reshape(blocks * xs, own, 2 * HD), BLOCK + ("x",))
    dkv_got = dkv_got.reshape(blocks, xs, own, 2 * HD)
    query_grad, key_grad, value_grad = finish(source, pieces, dkv_got)
    return (layer_output, query_grad, key_grad, value_grad, weight_grad)


def solution(mesh):
    split = Mesh(mesh.devices.reshape(2, 2, 2, 4, 4), ("zhi", "core", "zlo", "y", "x"))
    dp = ("zhi", "core")
    tokens = P(dp, ("zlo", "y", "x"), None)
    weight = P(("zhi", "core", "zlo", "y"), "x")
    columns = P(dp, BLOCK, "x")
    return jax.shard_map(
        shards,
        mesh=split,
        in_specs=(tokens, tokens, tokens, P(dp, None), weight, columns),
        out_specs=(columns, tokens, tokens, tokens, weight),
        check_vma=False,
    )
```

```python
import functools
import math

import jax
import jax.numpy as jnp
from jax import lax
from jax.experimental import pallas as pl
from jax.experimental.pallas import tpu as pltpu
from jax.sharding import Mesh
from jax.sharding import PartitionSpec as P

HD = 128
GROUP = 4
SEG = 256
SCALE = HD ** (-0.5)
LOG2_SCALE = SCALE * math.log2(math.e)
MASKED = -1e30
BF16 = jnp.bfloat16
F32 = jnp.float32
VMEM_LIMIT = 48 * 1024 * 1024
SHORT = pl.CostEstimate(flops=1, bytes_accessed=1, transcendentals=0)
PLANE = ("zhi", "zlo", "y")
BLOCK = ("zlo", "y")


def dot(a, b):
    return jnp.dot(a, b, preferred_element_type=F32)


def dot_nt(a, b):
    return lax.dot_general(a, b, (((1,), (1,)), ((), ())), preferred_element_type=F32)


def diagonal_mask():
    key_index = lax.broadcasted_iota(jnp.int32, (SEG, SEG), 0)
    query_index = lax.broadcasted_iota(jnp.int32, (SEG, SEG), 1)
    return key_index <= query_index


def pipeline(units, score, soften, mix):
    now = score(units[0])
    state = None
    for i in range(len(units) + 1):
        following = score(units[i + 1]) if i + 1 < len(units) else None
        if state is not None:
            mix(units[i - 1], state)
        if i < len(units):
            state = soften(units[i], now)
        now = following


def forward_kernel(order_ref, rank_ref, source_ref, *refs):
    pieces, (kv_ref, q_ref, att_t_ref, lse_ref, q_t, v_t, acc, peak, total) = refs[:-9], refs[-9:]
    own = pieces[0].shape[0]
    for i, piece in enumerate(pieces):
        place = pl.multiple_of(source_ref[i] * own, own)
        q_ref[pl.ds(place, own), :] = piece[...]
    runs = q_ref.shape[0] // SEG
    heads = q_ref.shape[1] // HD
    key_runs = kv_ref.shape[0] // SEG

    q_t[...] = q_ref[...].T

    @pl.loop(0, key_runs)
    def _(j):
        rows = pl.ds(pl.multiple_of(j * SEG, SEG), SEG)
        v_t[j] = kv_ref[rows, HD:].T

    for run in range(runs):
        cols = pl.ds(run * SEG, SEG)
        rank = rank_ref[run]

        def tiles(groups, first):
            units = [(g, h) for g in range(len(groups)) for h in range(heads)]
            keys = [
                [kv_ref[pl.ds(pl.multiple_of(j * SEG, SEG), SEG), :HD] for j in group]
                for group in groups
            ]
            values = [[v_t[j] for j in group] for group in groups]

            def score(unit):
                g, h = unit
                queries = q_t[pl.ds(h * HD, HD), cols]
                return [dot(k, queries) for k in keys[g]]

            def soften(unit, scores):
                g, h = unit
                if first and g == 0:
                    mask = diagonal_mask()
                    scores = [jnp.where(mask, s, MASKED) for s in scores]
                top = functools.reduce(
                    jnp.maximum, [jnp.max(s, axis=0, keepdims=True) for s in scores]
                )
                factor = None
                if not (first and g == 0):
                    old = peak[pl.ds(h, 1), :]
                    top = jnp.maximum(top, old)
                    factor = jnp.exp2((old - top) * LOG2_SCALE)
                peak[pl.ds(h, 1), :] = top
                shift = top * LOG2_SCALE
                weights = [jnp.exp2(s * LOG2_SCALE - shift) for s in scores]
                summed = functools.reduce(
                    jnp.add, [jnp.sum(w, axis=0, keepdims=True) for w in weights]
                )
                return factor, summed, [w.astype(BF16) for w in weights]

            def mix(unit, state):
                g, h = unit
                factor, summed, weights = state
                mixed = functools.reduce(
                    jnp.add, [dot(v, w) for v, w in zip(values[g], weights)]
                )
                if factor is None:
                    total[pl.ds(h, 1), :] = summed
                    acc[pl.ds(h * HD, HD), :] = mixed
                else:
                    total[pl.ds(h, 1), :] = total[pl.ds(h, 1), :] * factor + summed
                    acc[pl.ds(h * HD, HD), :] = acc[pl.ds(h * HD, HD), :] * factor + mixed

            pipeline(units, score, soften, mix)

        rest = rank % 4
        for left in range(4):

            @pl.when(rest == left)
            def _():
                groups = [[order_ref[rank]]]
                if left >= 2:
                    groups.append([order_ref[rank - 1], order_ref[rank - 2]])
                if left % 2:
                    groups.append([order_ref[rank - left]])
                tiles(groups, True)

        @pl.loop(0, rank // 4)
        def _(quad):
            start = 4 * quad
            tiles(
                [
                    [order_ref[start], order_ref[start + 1]],
                    [order_ref[start + 2], order_ref[start + 3]],
                ],
                False,
            )

        for h in range(heads):
            row_total = total[pl.ds(h, 1), :]
            lse_ref[pl.ds(h, 1), cols] = peak[pl.ds(h, 1), :] * LOG2_SCALE + jnp.log2(row_total)
            out = (acc[pl.ds(h * HD, HD), :] / row_total).astype(BF16)
            att_t_ref[pl.ds(h * HD, HD), cols] = out


def attend(order, rank, source, pieces, kv):
    own, width = pieces[0].shape
    rows = own * len(pieces)
    heads = width // HD
    length = kv.shape[0]
    smem = pl.BlockSpec(memory_space=pltpu.SMEM)
    vmem = pl.BlockSpec(memory_space=pltpu.VMEM)
    return pl.pallas_call(
        forward_kernel,
        name="attention_forward",
        out_shape=(
            jax.ShapeDtypeStruct((rows, width), BF16),
            jax.ShapeDtypeStruct((width, rows), BF16),
            jax.ShapeDtypeStruct((heads, rows), F32),
        ),
        in_specs=[smem, smem, smem] + [vmem] * (len(pieces) + 1),
        out_specs=(vmem, vmem, vmem),
        scratch_shapes=[
            pltpu.VMEM((width, rows), BF16),
            pltpu.VMEM((length // SEG, HD, SEG), BF16),
            pltpu.VMEM((width, SEG), F32),
            pltpu.VMEM((8, SEG), F32),
            pltpu.VMEM((8, SEG), F32),
        ],
        compiler_params=pltpu.CompilerParams(vmem_limit_bytes=VMEM_LIMIT),
        cost_estimate=pl.CostEstimate(
            flops=4 * rows * length * width,
            bytes_accessed=2 * (3 * rows * width + length * 2 * HD),
            transcendentals=rows * length * heads,
        ),
    )(order, rank, source, *pieces, kv)


def backward_kernel(
    rank_ref,
    key_rank_ref,
    q_ref,
    kv_ref,
    grad_t_ref,
    att_t_ref,
    lse_ref,
    dq_ref,
    dkv_ref,
    q_t,
    grad,
    delta,
    dq_t,
    dk,
    dv,
):
    runs = q_ref.shape[0] // SEG
    heads = q_ref.shape[1] // HD
    key_runs = kv_ref.shape[0] // SEG

    q_t[...] = q_ref[...].T
    grad[...] = grad_t_ref[...].T
    dq_t[...] = jnp.zeros_like(dq_t)
    for h in range(heads):
        part = pl.ds(h * HD, HD)
        delta[pl.ds(h, 1), :] = jnp.sum(
            grad_t_ref[part, :].astype(F32) * att_t_ref[part, :].astype(F32),
            axis=0,
            keepdims=True,
        )

    @pl.loop(0, key_runs)
    def _(j):
        rows = pl.ds(pl.multiple_of(j * SEG, SEG), SEG)
        key_rank = key_rank_ref[j]
        dk[...] = jnp.zeros_like(dk)
        dv[...] = jnp.zeros_like(dv)

        def tile(chosen, masked):
            keys = kv_ref[rows, :HD]
            values = kv_ref[rows, HD:]
            keys_t = keys.T
            sums = [dk[...], dv[...]]
            units = [(run, h) for run in chosen for h in range(heads)]

            def place(unit):
                return pl.ds(unit[1] * HD, HD), pl.ds(unit[0] * SEG, SEG)

            def score(unit):
                part, cols = place(unit)
                return dot(keys, q_t[part, cols]), dot(values, grad_t_ref[part, cols])

            def soften(unit, state):
                scores, prob_grad = state
                _, cols = place(unit)
                row = pl.ds(unit[1], 1)
                probs = jnp.exp2(scores * LOG2_SCALE - lse_ref[row, cols])
                if masked:
                    probs = jnp.where(diagonal_mask(), probs, 0.0)
                score_grad = (probs * (prob_grad - delta[row, cols])).astype(BF16)
                return probs.astype(BF16), score_grad

            def mix(unit, state):
                probs, score_grad = state
                part, cols = place(unit)
                dq_t[part, cols] += dot(keys_t, score_grad)
                sums[0] = sums[0] + dot(score_grad, q_ref[cols, part])
                sums[1] = sums[1] + dot(probs, grad[cols, part])

            pipeline(units, score, soften, mix)
            dk[...] = sums[0]
            dv[...] = sums[1]

        whole = [key_rank < rank_ref[run] for run in range(runs)]
        every = functools.reduce(jnp.logical_and, whole)
        pl.when(every)(functools.partial(tile, range(runs), False))
        for run in range(runs):
            alone = jnp.logical_and(whole[run], jnp.logical_not(every))
            pl.when(alone)(functools.partial(tile, [run], False))
            pl.when(key_rank == rank_ref[run])(functools.partial(tile, [run], True))
        dkv_ref[rows, :HD] = (dk[...] * SCALE).astype(BF16)
        dkv_ref[rows, HD:] = dv[...].astype(BF16)

    for run in range(runs):
        cols = pl.ds(run * SEG, SEG)
        for h in range(heads):
            part = pl.ds(h * HD, HD)
            dq_ref[cols, part] = (dq_t[part, cols] * SCALE).astype(BF16).T


def attend_back(rank, key_rank, q, kv, grad_t, att_t, lse):
    rows, width = q.shape
    heads = width // HD
    length = kv.shape[0]
    smem = pl.BlockSpec(memory_space=pltpu.SMEM)
    vmem = pl.BlockSpec(memory_space=pltpu.VMEM)
    return pl.pallas_call(
        backward_kernel,
        name="attention_backward",
        out_shape=(
            jax.ShapeDtypeStruct((rows, width), BF16),
            jax.ShapeDtypeStruct((length, 2 * HD), BF16),
        ),
        in_specs=[smem, smem] + [vmem] * 5,
        out_specs=(vmem, vmem),
        scratch_shapes=[
            pltpu.VMEM((width, rows), BF16),
            pltpu.VMEM((rows, width), BF16),
            pltpu.VMEM((8, rows), F32),
            pltpu.VMEM((width, rows), F32),
            pltpu.VMEM((SEG, HD), F32),
            pltpu.VMEM((SEG, HD), F32),
        ],
        compiler_params=pltpu.CompilerParams(vmem_limit_bytes=VMEM_LIMIT),
        cost_estimate=pl.CostEstimate(
            flops=10 * rows * length * width,
            bytes_accessed=2 * (4 * rows * width + 2 * length * 2 * HD),
            transcendentals=rows * length * heads,
        ),
    )(rank, key_rank, q, kv, grad_t, att_t, lse)


def pack_kernel(target_ref, q_ref, k_ref, v_ref, kv_ref, *pieces):
    width = pieces[0].shape[1]
    for i, piece in enumerate(pieces):
        columns = pl.ds(pl.multiple_of(target_ref[i] * width, width), width)
        piece[...] = q_ref[0, :, columns]
        kv_ref[i, :, :HD] = k_ref[0, :, pl.ds(i * HD, HD)]
        kv_ref[i, :, HD:] = v_ref[0, :, pl.ds(i * HD, HD)]


def pack(target, queries, key_vectors, value_vectors):
    own = queries.shape[1]
    parts = key_vectors.shape[2] // HD
    width = queries.shape[2] // parts
    smem = pl.BlockSpec(memory_space=pltpu.SMEM)
    vmem = pl.BlockSpec(memory_space=pltpu.VMEM)
    return pl.pallas_call(
        pack_kernel,
        name="pack_heads",
        in_specs=[smem, vmem, vmem, vmem],
        out_specs=(vmem,) * (parts + 1),
        out_shape=(jax.ShapeDtypeStruct((parts, own, 2 * HD), BF16),)
        + (jax.ShapeDtypeStruct((own, width), BF16),) * parts,
    )(target, queries, key_vectors, value_vectors)


def choose(mine, first, second, run):
    pl.when(mine)(functools.partial(run, first))
    pl.when(jnp.logical_not(mine))(functools.partial(run, second))


def fetch_weight(group_ref, core_ref, mine_ref, other_ref, slots, sems):
    for i in range(slots.shape[0]):
        group = group_ref[i]

        def start(weight, i=i, group=group):
            pltpu.make_async_copy(weight.at[group % 2], slots.at[i], sems.at[i]).start()

        choose(group // 2 == core_ref[0], mine_ref, other_ref, start)


def arrived(slots, sems, i):
    pltpu.make_async_copy(slots.at[i], slots.at[i], sems.at[i]).wait()
    return slots[i]


def fetch_columns(sources, slots, sems):
    *pieces, first, second = sources
    half = first.shape[0]
    last = len(pieces)
    copies = [
        pltpu.make_async_copy(piece.at[0], slots.at[i], sems.at[i]) for i, piece in enumerate(pieces)
    ]
    copies.append(pltpu.make_async_copy(first, slots.at[last, pl.ds(0, half)], sems.at[last]))
    copies.append(
        pltpu.make_async_copy(second, slots.at[last, pl.ds(half, half)], sems.at[last + 1])
    )
    for copy in copies:
        copy.start()
    return [[copy] for copy in copies[:last]] + [copies[last:]]


def grad_kernel(group_ref, core_ref, mine_ref, other_ref, *refs):
    *sources, out_ref, total, weights, columns, weight_sems, column_sems = refs
    fetch_weight(group_ref, core_ref, mine_ref, other_ref, weights, weight_sems)
    copies = fetch_columns(sources, columns, column_sems)
    for i, waits in enumerate(copies):
        weight = arrived(weights, weight_sems, i)
        for copy in waits:
            copy.wait()
        term = dot_nt(weight, columns[i])
        total[...] = term if i == 0 else total[...] + term
    out_ref[...] = total[...].astype(BF16)


def project_back(groups, core, mine, other, pieces):
    width, rows = mine.shape[1], pieces[0].shape[1]
    smem = pl.BlockSpec(memory_space=pltpu.SMEM)
    vmem = pl.BlockSpec(memory_space=pltpu.VMEM)
    far = pl.BlockSpec(memory_space=pl.ANY)
    count, columns = groups.shape[0], mine.shape[2]
    return pl.pallas_call(
        grad_kernel,
        name="attention_grad",
        in_specs=[smem, smem] + [far] * (2 + len(pieces)),
        out_specs=vmem,
        out_shape=jax.ShapeDtypeStruct((width, rows), BF16),
        scratch_shapes=[
            pltpu.VMEM((width, rows), F32),
            pltpu.VMEM((count, width, columns), BF16),
            pltpu.VMEM((count, rows, columns), BF16),
            pltpu.SemaphoreType.DMA((count,)),
            pltpu.SemaphoreType.DMA((count + 1,)),
        ],
        compiler_params=pltpu.CompilerParams(vmem_limit_bytes=VMEM_LIMIT),
        cost_estimate=SHORT,
    )(groups, core, mine, other, *pieces)


def weight_grad_kernel(group_ref, core_ref, att_t_ref, *refs):
    *sources, mine_ref, other_ref, columns, column_sems = refs
    copies = fetch_columns(sources, columns, column_sems)
    for i, waits in enumerate(copies):
        group = group_ref[i]
        for copy in waits:
            copy.wait()

        def product(out, i=i, group=group):
            out[group % 2] = dot(att_t_ref[...], columns[i]).astype(BF16)

        choose(group // 2 == core_ref[0], mine_ref, other_ref, product)


def weight_grad_parts(groups, core, att_t, pieces):
    count = groups.shape[0]
    out = jax.ShapeDtypeStruct((count // 2, att_t.shape[0], pieces[0].shape[2]), BF16)
    smem = pl.BlockSpec(memory_space=pltpu.SMEM)
    vmem = pl.BlockSpec(memory_space=pltpu.VMEM)
    far = pl.BlockSpec(memory_space=pl.ANY)
    return pl.pallas_call(
        weight_grad_kernel,
        name="weight_grad_parts",
        in_specs=[smem, smem, vmem] + [far] * len(pieces),
        out_specs=(vmem, vmem),
        out_shape=(out, out),
        scratch_shapes=[
            pltpu.VMEM((count, *pieces[0].shape[1:]), BF16),
            pltpu.SemaphoreType.DMA((count + 1,)),
        ],
        compiler_params=pltpu.CompilerParams(vmem_limit_bytes=VMEM_LIMIT),
        cost_estimate=SHORT,
    )(groups, core, att_t, *pieces)


def output_kernel(group_ref, core_ref, mine_ref, other_ref, att_t_ref, *refs):
    *outs, first, second, att, weights, weight_sems = refs
    half = first.shape[0]
    fetch_weight(group_ref, core_ref, mine_ref, other_ref, weights, weight_sems)
    att[...] = att_t_ref[...].T
    for i, out in enumerate(outs):
        out[...] = dot(att[...], arrived(weights, weight_sems, i)).astype(out.dtype)
    weight = arrived(weights, weight_sems, len(outs))
    first[...] = dot(att[:half, :], weight).astype(BF16)
    second[...] = dot(att[half:, :], weight).astype(BF16)


def project(groups, core, mine, other, att_t):
    count = groups.shape[0]
    width, rows = att_t.shape
    columns = mine.shape[2]
    smem = pl.BlockSpec(memory_space=pltpu.SMEM)
    vmem = pl.BlockSpec(memory_space=pltpu.VMEM)
    far = pl.BlockSpec(memory_space=pl.ANY)
    return pl.pallas_call(
        output_kernel,
        name="layer_output_parts",
        in_specs=[smem, smem, far, far, vmem],
        out_specs=(vmem,) * (count + 1),
        out_shape=(
            jax.ShapeDtypeStruct((rows, columns), F32),
            jax.ShapeDtypeStruct((rows, columns), BF16),
            jax.ShapeDtypeStruct((rows, columns), BF16),
            jax.ShapeDtypeStruct((rows // 2, columns), BF16),
            jax.ShapeDtypeStruct((rows // 2, columns), BF16),
        ),
        scratch_shapes=[
            pltpu.VMEM((rows, width), BF16),
            pltpu.VMEM((count, width, columns), BF16),
            pltpu.SemaphoreType.DMA((count,)),
        ],
        compiler_params=pltpu.CompilerParams(vmem_limit_bytes=VMEM_LIMIT),
        cost_estimate=SHORT,
    )(groups, core, mine, other, att_t)


def finish_kernel(source_ref, *refs):
    pieces, dkv_ref, (dq_ref, dk_ref, dv_ref) = refs[:-4], refs[-4], refs[-3:]
    width = pieces[0].shape[1]
    for i, piece in enumerate(pieces):
        columns = pl.ds(pl.multiple_of(source_ref[i] * width, width), width)
        dq_ref[0, :, columns] = piece[...]
    blocks, parts = dkv_ref.shape[:2]
    for u in range(parts):
        total = dkv_ref[0, u].astype(F32)
        for b in range(1, blocks):
            total = total + dkv_ref[b, u].astype(F32)
        total = total.astype(BF16)
        dk_ref[0, :, pl.ds(u * HD, HD)] = total[:, :HD]
        dv_ref[0, :, pl.ds(u * HD, HD)] = total[:, HD:]


def finish(source, pieces, dkv):
    own, width = pieces[0].shape
    parts = len(pieces)
    smem = pl.BlockSpec(memory_space=pltpu.SMEM)
    vmem = pl.BlockSpec(memory_space=pltpu.VMEM)
    return pl.pallas_call(
        finish_kernel,
        name="gather_gradients",
        in_specs=[smem] + [vmem] * (parts + 1),
        out_specs=(vmem, vmem, vmem),
        out_shape=(
            jax.ShapeDtypeStruct((1, own, parts * width), BF16),
            jax.ShapeDtypeStruct((1, own, parts * HD), BF16),
            jax.ShapeDtypeStruct((1, own, parts * HD), BF16),
        ),
        compiler_params=pltpu.CompilerParams(vmem_limit_bytes=VMEM_LIMIT),
    )(source, *pieces, dkv)


def exchange(array, axes):
    return lax.all_to_all(array, axes, split_axis=0, concat_axis=0, tiled=True)


def shift(array, axis, by):
    length = lax.axis_size(axis)
    return lax.ppermute(array, axis, [(i, (i + by) % length) for i in range(length)])


def pick(array, index):
    return lax.dynamic_index_in_dim(array, index, 0, keepdims=False)


def put(array, piece, index):
    return lax.dynamic_update_index_in_dim(array, piece, index, 0)


def spread(array, count):
    return jnp.broadcast_to(array[None], (count,) + array.shape).reshape(
        (count * array.shape[0],) + array.shape[1:]
    )


def swap_pairs():
    pairs = []
    for zhi in range(2):
        for core in range(2):
            for x in range(4):
                source = (zhi * 2 + core) * 4 + x
                target = ((x % 2) * 2 + x // 2) * 4 + zhi * 2 + core
                pairs.append((source, target))
    return pairs


def swap(array):
    return lax.ppermute(array, ("zhi", "core", "x"), swap_pairs())


def swap_back(array):
    return lax.ppermute(array, ("zhi", "core", "x"), [(b, a) for a, b in swap_pairs()])


def flip(array, by):
    return lax.ppermute(array, "x", [(i, i ^ by) for i in range(4)])


def after(array, *others):
    return lax.optimization_barrier((array,) + others)[0]


def shards(queries, key_vectors, value_vectors, positions, out_weight, out_grad):
    x = lax.axis_index("x")
    core = lax.axis_index("core")
    blk = lax.axis_index(BLOCK)
    xs = lax.axis_size("x")
    own = queries.shape[1]
    width = queries.shape[2] // xs
    blocks = lax.axis_size(BLOCK)
    rows = own * xs
    columns = out_grad.shape[2]

    key_rank = positions[0, ::SEG] // SEG
    count = key_rank.shape[0]
    index = jnp.arange(count, dtype=jnp.int32)
    order = jnp.sum(
        jnp.where(key_rank[None, :] == index[:, None], index[None, :], 0), axis=1
    ).astype(jnp.int32)
    rank = lax.dynamic_slice_in_dim(key_rank, blk * (rows // SEG), rows // SEG)

    steps = jnp.arange(xs, dtype=jnp.int32)
    target, source = (x + steps) % xs, (x - steps) % xs

    weight_swapped = swap(out_weight)
    kv_parts, *q_parts = pack(target, queries, key_vectors, value_vectors)
    q_pieces = q_parts[:1] + [shift(q_parts[d], "x", d) for d in range(1, xs)]
    kv = exchange(spread(kv_parts, blocks), BLOCK + ("x",)).reshape(blocks * rows, 2 * HD)

    near = jnp.stack([x, x ^ 1, x ^ 3, x ^ 2]).astype(jnp.int32)
    half = rows // 2
    og_own = after(out_grad, kv, weight_swapped, *q_pieces)
    og_1, og_3 = flip(og_own, 1), flip(og_own, 3)

    weight_swapped = after(weight_swapped, kv, *q_pieces)
    weight_half = exchange(spread(weight_swapped, 2 * blocks), PLANE)

    q, att_t, lse = attend(order, rank, source, q_pieces, kv)

    og_1, og_3, _ = lax.optimization_barrier((og_1, og_3, att_t))
    og = [out_grad, og_1, og_3, flip(og_1[0, :half], 3), flip(og_3[0, half:], 1)]

    weight_mine = after(weight_half, att_t).reshape(2, width, columns)
    weight_other = shift(weight_mine, "core", 1)

    cores = core.astype(jnp.int32).reshape(1)
    wg_mine, wg_sent = weight_grad_parts(near, cores, att_t, og)
    grad_t = project_back(near, cores, weight_mine, weight_other, og)

    wg_got = after(shift(wg_sent, "core", 1), grad_t)
    wg_half = (wg_mine.astype(F32) + wg_got.astype(F32)).astype(BF16)
    wg_half = wg_half.reshape(2 * blocks, width // blocks, columns)
    wg_parts = exchange(wg_half, PLANE)
    weight_grad = swap_back(jnp.sum(wg_parts.astype(F32), axis=0))

    lo, lo_1, lo_3, lo_first, lo_second = project(near, cores, weight_mine, weight_other, att_t)
    lo_3 = lo_3.at[:half].add(flip(lo_first, 1))
    lo_1 = lo_1.at[half:].add(flip(lo_second, 3))
    lo = lo + flip(lo_1, 1).astype(F32) + flip(lo_3, 3).astype(F32)
    layer_output = lo.astype(BF16)[None]

    grad_t = after(grad_t, wg_half, lo_1, lo_3)
    dq, dkv = attend_back(rank, key_rank, q, kv, grad_t, att_t, lse)

    dkv = after(dkv, layer_output)
    dq_parts = dq.reshape(xs, own, width)
    pieces = [pick(dq_parts, x)]
    for d in range(1, xs):
        pieces.append(shift(pick(dq_parts, (x + d) % xs), "x", d))
    dkv_got = exchange(dkv.reshape(blocks * xs, own, 2 * HD), BLOCK + ("x",))
    dkv_got = dkv_got.reshape(blocks, xs, own, 2 * HD)
    query_grad, key_grad, value_grad = finish(source, pieces, dkv_got)
    return (layer_output, query_grad, key_grad, value_grad, weight_grad)


def solution(mesh):
    split = Mesh(mesh.devices.reshape(2, 2, 2, 4, 4), ("zhi", "core", "zlo", "y", "x"))
    dp = ("zhi", "core")
    tokens = P(dp, ("zlo", "y", "x"), None)
    weight = P(("zhi", "core", "zlo", "y"), "x")
    columns = P(dp, BLOCK, "x")
    return jax.shard_map(
        shards,
        mesh=split,
        in_specs=(tokens, tokens, tokens, P(dp, None), weight, columns),
        out_specs=(columns, tokens, tokens, tokens, weight),
        check_vma=False,
    )
```

```python
import functools
import math

import jax
import jax.numpy as jnp
from jax import lax
from jax.experimental import pallas as pl
from jax.experimental.pallas import tpu as pltpu
from jax.sharding import Mesh
from jax.sharding import PartitionSpec as P

HD = 128
GROUP = 4
SEG = 256
SCALE = HD ** (-0.5)
LOG2_SCALE = SCALE * math.log2(math.e)
MASKED = -1e30
BF16 = jnp.bfloat16
F32 = jnp.float32
VMEM_LIMIT = 24 * 1024 * 1024
SHORT = pl.CostEstimate(flops=1, bytes_accessed=1, transcendentals=0)
PLANE = ("zhi", "zlo", "y")
BLOCK = ("zlo", "y")


def dot(a, b):
    return jnp.dot(a, b, preferred_element_type=F32)


def dot_nt(a, b):
    return lax.dot_general(a, b, (((1,), (1,)), ((), ())), preferred_element_type=F32)


def diagonal_mask():
    key_index = lax.broadcasted_iota(jnp.int32, (SEG, SEG), 0)
    query_index = lax.broadcasted_iota(jnp.int32, (SEG, SEG), 1)
    return key_index <= query_index


def pipeline(units, score, soften, mix):
    now = score(units[0])
    state = None
    for i in range(len(units) + 1):
        following = score(units[i + 1]) if i + 1 < len(units) else None
        if state is not None:
            mix(units[i - 1], state)
        if i < len(units):
            state = soften(units[i], now)
        now = following


def forward_kernel(order_ref, rank_ref, source_ref, *refs):
    pieces, (kv_ref, q_ref, att_t_ref, lse_ref, q_t, v_t, acc, peak, total) = refs[:-9], refs[-9:]
    own = pieces[0].shape[0]
    for i, piece in enumerate(pieces):
        place = pl.multiple_of(source_ref[i] * own, own)
        q_ref[pl.ds(place, own), :] = piece[...]
    runs = q_ref.shape[0] // SEG
    heads = q_ref.shape[1] // HD
    key_runs = kv_ref.shape[0] // SEG

    q_t[...] = q_ref[...].T

    @pl.loop(0, key_runs)
    def _(j):
        rows = pl.ds(pl.multiple_of(j * SEG, SEG), SEG)
        v_t[j] = kv_ref[rows, HD:].T

    for run in range(runs):
        cols = pl.ds(run * SEG, SEG)
        rank = rank_ref[run]

        def tiles(groups, first):
            units = [(g, h) for g in range(len(groups)) for h in range(heads)]
            keys = [
                [kv_ref[pl.ds(pl.multiple_of(j * SEG, SEG), SEG), :HD] for j in group]
                for group in groups
            ]
            values = [[v_t[j] for j in group] for group in groups]

            def score(unit):
                g, h = unit
                queries = q_t[pl.ds(h * HD, HD), cols]
                return [dot(k, queries) for k in keys[g]]

            def soften(unit, scores):
                g, h = unit
                if first and g == 0:
                    mask = diagonal_mask()
                    scores = [jnp.where(mask, s, MASKED) for s in scores]
                top = functools.reduce(
                    jnp.maximum, [jnp.max(s, axis=0, keepdims=True) for s in scores]
                )
                factor = None
                if not (first and g == 0):
                    old = peak[pl.ds(h, 1), :]
                    top = jnp.maximum(top, old)
                    factor = jnp.exp2((old - top) * LOG2_SCALE)
                peak[pl.ds(h, 1), :] = top
                shift = top * LOG2_SCALE
                weights = [jnp.exp2(s * LOG2_SCALE - shift) for s in scores]
                summed = functools.reduce(
                    jnp.add, [jnp.sum(w, axis=0, keepdims=True) for w in weights]
                )
                return factor, summed, [w.astype(BF16) for w in weights]

            def mix(unit, state):
                g, h = unit
                factor, summed, weights = state
                mixed = functools.reduce(
                    jnp.add, [dot(v, w) for v, w in zip(values[g], weights)]
                )
                if factor is None:
                    total[pl.ds(h, 1), :] = summed
                    acc[pl.ds(h * HD, HD), :] = mixed
                else:
                    total[pl.ds(h, 1), :] = total[pl.ds(h, 1), :] * factor + summed
                    acc[pl.ds(h * HD, HD), :] = acc[pl.ds(h * HD, HD), :] * factor + mixed

            pipeline(units, score, soften, mix)

        rest = rank % 4
        for left in range(4):

            @pl.when(rest == left)
            def _():
                groups = [[order_ref[rank]]]
                if left >= 2:
                    groups.append([order_ref[rank - 1], order_ref[rank - 2]])
                if left % 2:
                    groups.append([order_ref[rank - left]])
                tiles(groups, True)

        @pl.loop(0, rank // 4)
        def _(quad):
            start = 4 * quad
            tiles(
                [
                    [order_ref[start], order_ref[start + 1]],
                    [order_ref[start + 2], order_ref[start + 3]],
                ],
                False,
            )

        for h in range(heads):
            row_total = total[pl.ds(h, 1), :]
            lse_ref[pl.ds(h, 1), cols] = peak[pl.ds(h, 1), :] * LOG2_SCALE + jnp.log2(row_total)
            out = (acc[pl.ds(h * HD, HD), :] / row_total).astype(BF16)
            att_t_ref[pl.ds(h * HD, HD), cols] = out


def attend(order, rank, source, pieces, kv):
    own, width = pieces[0].shape
    rows = own * len(pieces)
    heads = width // HD
    length = kv.shape[0]
    smem = pl.BlockSpec(memory_space=pltpu.SMEM)
    vmem = pl.BlockSpec(memory_space=pltpu.VMEM)
    return pl.pallas_call(
        forward_kernel,
        name="attention_forward",
        out_shape=(
            jax.ShapeDtypeStruct((rows, width), BF16),
            jax.ShapeDtypeStruct((width, rows), BF16),
            jax.ShapeDtypeStruct((heads, rows), F32),
        ),
        in_specs=[smem, smem, smem] + [vmem] * (len(pieces) + 1),
        out_specs=(vmem, vmem, vmem),
        scratch_shapes=[
            pltpu.VMEM((width, rows), BF16),
            pltpu.VMEM((length // SEG, HD, SEG), BF16),
            pltpu.VMEM((width, SEG), F32),
            pltpu.VMEM((8, SEG), F32),
            pltpu.VMEM((8, SEG), F32),
        ],
        compiler_params=pltpu.CompilerParams(vmem_limit_bytes=VMEM_LIMIT),
        cost_estimate=pl.CostEstimate(
            flops=4 * rows * length * width,
            bytes_accessed=2 * (3 * rows * width + length * 2 * HD),
            transcendentals=rows * length * heads,
        ),
    )(order, rank, source, *pieces, kv)


def backward_kernel(
    rank_ref,
    key_rank_ref,
    q_ref,
    kv_ref,
    grad_t_ref,
    att_t_ref,
    lse_ref,
    dq_ref,
    dkv_ref,
    q_t,
    grad,
    delta,
    dq_t,
    dk,
    dv,
):
    runs = q_ref.shape[0] // SEG
    heads = q_ref.shape[1] // HD
    key_runs = kv_ref.shape[0] // SEG

    q_t[...] = q_ref[...].T
    grad[...] = grad_t_ref[...].T
    dq_t[...] = jnp.zeros_like(dq_t)
    for h in range(heads):
        part = pl.ds(h * HD, HD)
        delta[pl.ds(h, 1), :] = jnp.sum(
            grad_t_ref[part, :].astype(F32) * att_t_ref[part, :].astype(F32),
            axis=0,
            keepdims=True,
        )

    @pl.loop(0, key_runs)
    def _(j):
        rows = pl.ds(pl.multiple_of(j * SEG, SEG), SEG)
        key_rank = key_rank_ref[j]
        dk[...] = jnp.zeros_like(dk)
        dv[...] = jnp.zeros_like(dv)

        def tile(chosen, masked):
            keys = kv_ref[rows, :HD]
            values = kv_ref[rows, HD:]
            keys_t = keys.T
            sums = [dk[...], dv[...]]
            units = [(run, h) for run in chosen for h in range(heads)]

            def place(unit):
                return pl.ds(unit[1] * HD, HD), pl.ds(unit[0] * SEG, SEG)

            def score(unit):
                part, cols = place(unit)
                return dot(keys, q_t[part, cols]), dot(values, grad_t_ref[part, cols])

            def soften(unit, state):
                scores, prob_grad = state
                _, cols = place(unit)
                row = pl.ds(unit[1], 1)
                probs = jnp.exp2(scores * LOG2_SCALE - lse_ref[row, cols])
                if masked:
                    probs = jnp.where(diagonal_mask(), probs, 0.0)
                score_grad = (probs * (prob_grad - delta[row, cols])).astype(BF16)
                return probs.astype(BF16), score_grad

            def mix(unit, state):
                probs, score_grad = state
                part, cols = place(unit)
                dq_t[part, cols] += dot(keys_t, score_grad)
                sums[0] = sums[0] + dot(score_grad, q_ref[cols, part])
                sums[1] = sums[1] + dot(probs, grad[cols, part])

            pipeline(units, score, soften, mix)
            dk[...] = sums[0]
            dv[...] = sums[1]

        whole = [key_rank < rank_ref[run] for run in range(runs)]
        every = functools.reduce(jnp.logical_and, whole)
        pl.when(every)(functools.partial(tile, range(runs), False))
        for run in range(runs):
            alone = jnp.logical_and(whole[run], jnp.logical_not(every))
            pl.when(alone)(functools.partial(tile, [run], False))
            pl.when(key_rank == rank_ref[run])(functools.partial(tile, [run], True))
        dkv_ref[rows, :HD] = (dk[...] * SCALE).astype(BF16)
        dkv_ref[rows, HD:] = dv[...].astype(BF16)

    for run in range(runs):
        cols = pl.ds(run * SEG, SEG)
        for h in range(heads):
            part = pl.ds(h * HD, HD)
            dq_ref[cols, part] = (dq_t[part, cols] * SCALE).astype(BF16).T


def attend_back(rank, key_rank, q, kv, grad_t, att_t, lse):
    rows, width = q.shape
    heads = width // HD
    length = kv.shape[0]
    smem = pl.BlockSpec(memory_space=pltpu.SMEM)
    vmem = pl.BlockSpec(memory_space=pltpu.VMEM)
    return pl.pallas_call(
        backward_kernel,
        name="attention_backward",
        out_shape=(
            jax.ShapeDtypeStruct((rows, width), BF16),
            jax.ShapeDtypeStruct((length, 2 * HD), BF16),
        ),
        in_specs=[smem, smem] + [vmem] * 5,
        out_specs=(vmem, vmem),
        scratch_shapes=[
            pltpu.VMEM((width, rows), BF16),
            pltpu.VMEM((rows, width), BF16),
            pltpu.VMEM((8, rows), F32),
            pltpu.VMEM((width, rows), F32),
            pltpu.VMEM((SEG, HD), F32),
            pltpu.VMEM((SEG, HD), F32),
        ],
        compiler_params=pltpu.CompilerParams(vmem_limit_bytes=VMEM_LIMIT),
        cost_estimate=pl.CostEstimate(
            flops=10 * rows * length * width,
            bytes_accessed=2 * (4 * rows * width + 2 * length * 2 * HD),
            transcendentals=rows * length * heads,
        ),
    )(rank, key_rank, q, kv, grad_t, att_t, lse)


def pack_kernel(target_ref, q_ref, k_ref, v_ref, kv_ref, *pieces):
    width = pieces[0].shape[1]
    for i, piece in enumerate(pieces):
        columns = pl.ds(pl.multiple_of(target_ref[i] * width, width), width)
        piece[...] = q_ref[0, :, columns]
        for block in range(kv_ref.shape[0]):
            kv_ref[block, i, :, :HD] = k_ref[0, :, pl.ds(i * HD, HD)]
            kv_ref[block, i, :, HD:] = v_ref[0, :, pl.ds(i * HD, HD)]


def pack(blocks, target, queries, key_vectors, value_vectors):
    own = queries.shape[1]
    parts = key_vectors.shape[2] // HD
    width = queries.shape[2] // parts
    smem = pl.BlockSpec(memory_space=pltpu.SMEM)
    vmem = pl.BlockSpec(memory_space=pltpu.VMEM)
    return pl.pallas_call(
        pack_kernel,
        name="pack_heads",
        in_specs=[smem, vmem, vmem, vmem],
        out_specs=(vmem,) * (parts + 1),
        out_shape=(jax.ShapeDtypeStruct((blocks, parts, own, 2 * HD), BF16),)
        + (jax.ShapeDtypeStruct((own, width), BF16),) * parts,
    )(target, queries, key_vectors, value_vectors)


def choose(mine, first, second, run):
    pl.when(mine)(functools.partial(run, first))
    pl.when(jnp.logical_not(mine))(functools.partial(run, second))


def fetch_weight(group_ref, core_ref, mine_ref, other_ref, slots, sems):
    for i in range(slots.shape[0]):
        group = group_ref[i]

        def start(weight, i=i, group=group):
            pltpu.make_async_copy(weight.at[group % 2], slots.at[i], sems.at[i]).start()

        choose(group // 2 == core_ref[0], mine_ref, other_ref, start)


def arrived(slots, sems, i):
    pltpu.make_async_copy(slots.at[i], slots.at[i], sems.at[i]).wait()
    return slots[i]


def fetch_columns(sources, slots, sems):
    *pieces, first, second = sources
    half = first.shape[0]
    last = len(pieces)
    copies = [
        pltpu.make_async_copy(piece.at[0], slots.at[i], sems.at[i]) for i, piece in enumerate(pieces)
    ]
    copies.append(pltpu.make_async_copy(first, slots.at[last, pl.ds(0, half)], sems.at[last]))
    copies.append(
        pltpu.make_async_copy(second, slots.at[last, pl.ds(half, half)], sems.at[last + 1])
    )
    for copy in copies:
        copy.start()
    return [[copy] for copy in copies[:last]] + [copies[last:]]


def grad_kernel(group_ref, core_ref, mine_ref, other_ref, *refs):
    *sources, out_ref, total, weights, columns, weight_sems, column_sems = refs
    fetch_weight(group_ref, core_ref, mine_ref, other_ref, weights, weight_sems)
    copies = fetch_columns(sources, columns, column_sems)
    for i, waits in enumerate(copies):
        weight = arrived(weights, weight_sems, i)
        for copy in waits:
            copy.wait()
        term = dot_nt(weight, columns[i])
        total[...] = term if i == 0 else total[...] + term
    out_ref[...] = total[...].astype(BF16)


def project_back(groups, core, mine, other, pieces):
    width, rows = mine.shape[1], pieces[0].shape[1]
    smem = pl.BlockSpec(memory_space=pltpu.SMEM)
    vmem = pl.BlockSpec(memory_space=pltpu.VMEM)
    far = pl.BlockSpec(memory_space=pl.ANY)
    count, columns = groups.shape[0], mine.shape[2]
    return pl.pallas_call(
        grad_kernel,
        name="attention_grad",
        in_specs=[smem, smem] + [far] * (2 + len(pieces)),
        out_specs=vmem,
        out_shape=jax.ShapeDtypeStruct((width, rows), BF16),
        scratch_shapes=[
            pltpu.VMEM((width, rows), F32),
            pltpu.VMEM((count, width, columns), BF16),
            pltpu.VMEM((count, rows, columns), BF16),
            pltpu.SemaphoreType.DMA((count,)),
            pltpu.SemaphoreType.DMA((count + 1,)),
        ],
        compiler_params=pltpu.CompilerParams(vmem_limit_bytes=VMEM_LIMIT),
        cost_estimate=SHORT,
    )(groups, core, mine, other, *pieces)


def weight_grad_kernel(group_ref, core_ref, att_t_ref, *refs):
    *sources, mine_ref, other_ref, columns, column_sems = refs
    copies = fetch_columns(sources, columns, column_sems)
    for i, waits in enumerate(copies):
        group = group_ref[i]
        for copy in waits:
            copy.wait()

        def product(out, i=i, group=group):
            out[group % 2] = dot(att_t_ref[...], columns[i]).astype(BF16)

        choose(group // 2 == core_ref[0], mine_ref, other_ref, product)


def weight_grad_parts(groups, core, att_t, pieces):
    count = groups.shape[0]
    out = jax.ShapeDtypeStruct((count // 2, att_t.shape[0], pieces[0].shape[2]), BF16)
    smem = pl.BlockSpec(memory_space=pltpu.SMEM)
    vmem = pl.BlockSpec(memory_space=pltpu.VMEM)
    far = pl.BlockSpec(memory_space=pl.ANY)
    return pl.pallas_call(
        weight_grad_kernel,
        name="weight_grad_parts",
        in_specs=[smem, smem, vmem] + [far] * len(pieces),
        out_specs=(vmem, vmem),
        out_shape=(out, out),
        scratch_shapes=[
            pltpu.VMEM((count, *pieces[0].shape[1:]), BF16),
            pltpu.SemaphoreType.DMA((count + 1,)),
        ],
        compiler_params=pltpu.CompilerParams(vmem_limit_bytes=VMEM_LIMIT),
        cost_estimate=SHORT,
    )(groups, core, att_t, *pieces)


def output_kernel(group_ref, core_ref, mine_ref, other_ref, att_t_ref, *refs):
    *outs, first, second, att, weights, weight_sems = refs
    half = first.shape[0]
    fetch_weight(group_ref, core_ref, mine_ref, other_ref, weights, weight_sems)
    att[...] = att_t_ref[...].T
    for i, out in enumerate(outs):
        out[...] = dot(att[...], arrived(weights, weight_sems, i)).astype(out.dtype)
    weight = arrived(weights, weight_sems, len(outs))
    first[...] = dot(att[:half, :], weight).astype(BF16)
    second[...] = dot(att[half:, :], weight).astype(BF16)


def project(groups, core, mine, other, att_t):
    count = groups.shape[0]
    width, rows = att_t.shape
    columns = mine.shape[2]
    smem = pl.BlockSpec(memory_space=pltpu.SMEM)
    vmem = pl.BlockSpec(memory_space=pltpu.VMEM)
    far = pl.BlockSpec(memory_space=pl.ANY)
    return pl.pallas_call(
        output_kernel,
        name="layer_output_parts",
        in_specs=[smem, smem, far, far, vmem],
        out_specs=(vmem,) * (count + 1),
        out_shape=(
            jax.ShapeDtypeStruct((rows, columns), F32),
            jax.ShapeDtypeStruct((rows, columns), BF16),
            jax.ShapeDtypeStruct((rows, columns), BF16),
            jax.ShapeDtypeStruct((rows // 2, columns), BF16),
            jax.ShapeDtypeStruct((rows // 2, columns), BF16),
        ),
        scratch_shapes=[
            pltpu.VMEM((rows, width), BF16),
            pltpu.VMEM((count, width, columns), BF16),
            pltpu.SemaphoreType.DMA((count,)),
        ],
        compiler_params=pltpu.CompilerParams(vmem_limit_bytes=VMEM_LIMIT),
        cost_estimate=SHORT,
    )(groups, core, mine, other, att_t)


def finish_kernel(source_ref, *refs):
    pieces, dkv_ref, (dq_ref, dk_ref, dv_ref) = refs[:-4], refs[-4], refs[-3:]
    width = pieces[0].shape[1]
    for i, piece in enumerate(pieces):
        columns = pl.ds(pl.multiple_of(source_ref[i] * width, width), width)
        dq_ref[0, :, columns] = piece[...]
    blocks, parts = dkv_ref.shape[:2]
    for u in range(parts):
        total = dkv_ref[0, u].astype(F32)
        for b in range(1, blocks):
            total = total + dkv_ref[b, u].astype(F32)
        total = total.astype(BF16)
        dk_ref[0, :, pl.ds(u * HD, HD)] = total[:, :HD]
        dv_ref[0, :, pl.ds(u * HD, HD)] = total[:, HD:]


def finish(source, pieces, dkv):
    own, width = pieces[0].shape
    parts = len(pieces)
    smem = pl.BlockSpec(memory_space=pltpu.SMEM)
    vmem = pl.BlockSpec(memory_space=pltpu.VMEM)
    return pl.pallas_call(
        finish_kernel,
        name="gather_gradients",
        in_specs=[smem] + [vmem] * (parts + 1),
        out_specs=(vmem, vmem, vmem),
        out_shape=(
            jax.ShapeDtypeStruct((1, own, parts * width), BF16),
            jax.ShapeDtypeStruct((1, own, parts * HD), BF16),
            jax.ShapeDtypeStruct((1, own, parts * HD), BF16),
        ),
        compiler_params=pltpu.CompilerParams(vmem_limit_bytes=VMEM_LIMIT),
    )(source, *pieces, dkv)


def exchange(array, axes):
    return lax.all_to_all(array, axes, split_axis=0, concat_axis=0, tiled=True)


def shift(array, axis, by):
    length = lax.axis_size(axis)
    return lax.ppermute(array, axis, [(i, (i + by) % length) for i in range(length)])


def pick(array, index):
    return lax.dynamic_index_in_dim(array, index, 0, keepdims=False)


def put(array, piece, index):
    return lax.dynamic_update_index_in_dim(array, piece, index, 0)


def spread(array, count):
    return jnp.broadcast_to(array[None], (count,) + array.shape).reshape(
        (count * array.shape[0],) + array.shape[1:]
    )


def swap_pairs():
    pairs = []
    for zhi in range(2):
        for core in range(2):
            for x in range(4):
                source = (zhi * 2 + core) * 4 + x
                target = ((x % 2) * 2 + x // 2) * 4 + zhi * 2 + core
                pairs.append((source, target))
    return pairs


def swap(array):
    return lax.ppermute(array, ("zhi", "core", "x"), swap_pairs())


def swap_back(array):
    return lax.ppermute(array, ("zhi", "core", "x"), [(b, a) for a, b in swap_pairs()])


def flip(array, by):
    return lax.ppermute(array, "x", [(i, i ^ by) for i in range(4)])


def after(array, *others):
    return lax.optimization_barrier((array,) + others)[0]


def shards(queries, key_vectors, value_vectors, positions, out_weight, out_grad):
    x = lax.axis_index("x")
    core = lax.axis_index("core")
    blk = lax.axis_index(BLOCK)
    xs = lax.axis_size("x")
    own = queries.shape[1]
    width = queries.shape[2] // xs
    blocks = lax.axis_size(BLOCK)
    rows = own * xs
    columns = out_grad.shape[2]

    key_rank = positions[0, ::SEG] // SEG
    count = key_rank.shape[0]
    index = jnp.arange(count, dtype=jnp.int32)
    order = jnp.sum(
        jnp.where(key_rank[None, :] == index[:, None], index[None, :], 0), axis=1
    ).astype(jnp.int32)
    rank = lax.dynamic_slice_in_dim(key_rank, blk * (rows // SEG), rows // SEG)

    steps = jnp.arange(xs, dtype=jnp.int32)
    target, source = (x + steps) % xs, (x - steps) % xs

    weight_swapped = swap(out_weight)
    kv_parts, *q_parts = pack(blocks, target, queries, key_vectors, value_vectors)
    q_pieces = q_parts[:1] + [shift(q_parts[d], "x", d) for d in range(1, xs)]
    kv_parts = kv_parts.reshape(blocks * xs, own, 2 * HD)
    kv = exchange(kv_parts, BLOCK + ("x",)).reshape(blocks * rows, 2 * HD)

    near = jnp.stack([x, x ^ 1, x ^ 3, x ^ 2]).astype(jnp.int32)
    half = rows // 2
    og_own = after(out_grad, kv, weight_swapped, *q_pieces)
    og_1, og_3 = flip(og_own, 1), flip(og_own, 3)

    weight_swapped = after(weight_swapped, kv, *q_pieces)
    weight_half = exchange(spread(weight_swapped, 2 * blocks), PLANE)

    q, att_t, lse = attend(order, rank, source, q_pieces, kv)

    og_1, og_3, _ = lax.optimization_barrier((og_1, og_3, att_t))
    og = [out_grad, og_1, og_3, flip(og_1[0, :half], 3), flip(og_3[0, half:], 1)]

    weight_mine = after(weight_half, att_t).reshape(2, width, columns)
    weight_other = shift(weight_mine, "core", 1)

    cores = core.astype(jnp.int32).reshape(1)
    wg_mine, wg_sent = weight_grad_parts(near, cores, att_t, og)
    grad_t = project_back(near, cores, weight_mine, weight_other, og)

    wg_got = after(shift(wg_sent, "core", 1), grad_t)
    wg_half = (wg_mine.astype(F32) + wg_got.astype(F32)).astype(BF16)
    wg_half = wg_half.reshape(2 * blocks, width // blocks, columns)
    wg_parts = exchange(wg_half, PLANE)
    weight_grad = swap_back(jnp.sum(wg_parts.astype(F32), axis=0))

    lo, lo_1, lo_3, lo_first, lo_second = project(near, cores, weight_mine, weight_other, att_t)
    lo_3 = lo_3.at[:half].add(flip(lo_first, 1))
    lo_1 = lo_1.at[half:].add(flip(lo_second, 3))
    lo = lo + flip(lo_1, 1).astype(F32) + flip(lo_3, 3).astype(F32)
    layer_output = lo.astype(BF16)[None]

    grad_t = after(grad_t, wg_half, lo_1, lo_3)
    dq, dkv = attend_back(rank, key_rank, q, kv, grad_t, att_t, lse)

    dkv = after(dkv, layer_output)
    dq_parts = dq.reshape(xs, own, width)
    pieces = [pick(dq_parts, x)]
    for d in range(1, xs):
        pieces.append(shift(pick(dq_parts, (x + d) % xs), "x", d))
    dkv_got = exchange(dkv.reshape(blocks * xs, own, 2 * HD), BLOCK + ("x",))
    dkv_got = dkv_got.reshape(blocks, xs, own, 2 * HD)
    query_grad, key_grad, value_grad = finish(source, pieces, dkv_got)
    return (layer_output, query_grad, key_grad, value_grad, weight_grad)


def solution(mesh):
    split = Mesh(mesh.devices.reshape(2, 2, 2, 4, 4), ("zhi", "core", "zlo", "y", "x"))
    dp = ("zhi", "core")
    tokens = P(dp, ("zlo", "y", "x"), None)
    weight = P(("zhi", "core", "zlo", "y"), "x")
    columns = P(dp, BLOCK, "x")
    return jax.shard_map(
        shards,
        mesh=split,
        in_specs=(tokens, tokens, tokens, P(dp, None), weight, columns),
        out_specs=(columns, tokens, tokens, tokens, weight),
        check_vma=False,
    )
```
